256 devices in a mesh: ctx: 32 (over x, z_lo, core), tp: 8 (over y, z_hi).
Axes of the slice: x: 4, y: 4, z: 8 (z_hi: 2, z_lo: 4; z = z_hi * 4 + z_lo), core: 2. Of those that a mesh axis runs over, the one named last changes fastest.
Arguments:
- query: bfloat16 [16384, 3072], P('ctx', 'tp'), may hold values from -32 to 32
- keys: bfloat16 [16384, 3072], P('ctx', 'tp'), may hold values from -12 to 12
- values: bfloat16 [16384, 3072], P('ctx', 'tp'), may hold values from -6 to 6
- image_ids: int32 [16384], P('ctx'), may hold values from 0 to 31, never falling along the last dimension, each value on 1 to 1024 neighbouring positions
- out_weight: bfloat16 [3072, 3072], P('tp'), may hold values from -0.109375 to 0.109375
- cotangent: bfloat16 [16384, 3072], P('ctx', 'tp'), may hold values from -6 to 6
Outputs:
- mixed: bfloat16 [16384, 3072], P('ctx', 'tp')
- grad_query: bfloat16 [16384, 3072], P('ctx', 'tp')
- grad_keys: bfloat16 [16384, 3072], P('ctx', 'tp')
- grad_values: bfloat16 [16384, 3072], P('ctx', 'tp')
- grad_weight: bfloat16 [3072, 3072], P('tp')
The draws below stay inside these ranges and needn't reach their ends.
Inputs may be any that keep to these rules, and one draw needn't show every extreme that they name: `image_ids`: never falls along the tokens; each image holds 1 to 1024 consecutive tokens and some image exactly 1024.
All inputs are finite; a program needn't handle non-finite values.
Results may differ from the reference program's by a relative error of at most 0.012.
Values may be sent and summed in bfloat16 or wider, within the bound.
A program may use at most 128 MiB of HBM per device.

```python
import math
import jax
import jax.numpy as jnp
import numpy as np
from jax import lax

D = 3072
HEADS = 24
HEAD_DIM = 128
TOK_DEV = 512
IMG_MAX = 1024
TOKENS = 16384
N_CTX = 32


def draw_query(key, part):
    key = jax.random.fold_in(key, 11)
    first = jax.random.fold_in(key, 0)
    own_rows = jnp.clip(jax.random.normal(first, (TOKENS, HEADS * HEAD_DIM), jnp.float32), -4.0, 4.0)
    out = own_rows
    return out.astype(jnp.bfloat16)


def draw_keys(key, part):
    key = jax.random.fold_in(key, 23)
    own_rows = jnp.clip(jax.random.normal(key, (TOKENS, HEADS * HEAD_DIM), jnp.float32), -4.0, 4.0)
    out = own_rows
    return out.astype(jnp.bfloat16)


def block_scale(rng, dims, pieces, smallest, top_value):
    loudness, own = 1.0, jax.random.fold_in(rng, 6)
    for position, shards_of in pieces:
        draws = jnp.exp(jax.random.uniform(jax.random.fold_in(own, position), (shards_of,), jnp.float32, smallest / len(pieces), top_value / len(pieces)))
        loudness = loudness * jnp.repeat(draws, dims[position] // shards_of).reshape([-1 if axis == position else 1 for axis in range(len(dims))])
    return loudness


def length_profile(number_of, total, bound, skew):
    portions = [(1 << 20) // math.isqrt(grade ** skew) + 1 for grade in range(2, number_of + 1)]
    rest, holding = total - bound - (number_of - 1), [1] * (number_of - 1)
    while rest > 0:
        candidates = [i for i in range(number_of - 1) if holding[i] < bound]
        pool, left = sum([portions[i] for i in candidates]), rest
        for i in candidates:
            addition = min(bound - holding[i], max(1, left * portions[i] // pool), rest)
            holding[i] = holding[i] + addition
            rest = rest - addition
    return np.array([bound] + holding)


def ragged_sizes(key, amount, total, limit, lean):
    if amount == 2:
        one = jax.random.randint(key, (), max(1, total - limit), min(limit, total - 1) + 1)
        return jnp.stack([one, total - one])
    tallies = jnp.asarray(length_profile(amount, total, limit, lean), jnp.int32)
    couples = (amount - 1) // 2
    giver, receiver = tallies[1:1 + 2 * couples:2], tallies[2:2 + 2 * couples:2]
    margin = jnp.minimum(giver - 1, limit - receiver)
    shifted = jax.random.randint(jax.random.fold_in(key, 1), (couples,), 0, 1 << 20) % (margin + 1)
    tallies = tallies.at[1:1 + 2 * couples:2].set(giver - shifted).at[2:2 + 2 * couples:2].set(receiver + shifted)
    return tallies[jax.random.permutation(jax.random.fold_in(key, 2), amount)]


def scatter_about(own_key, shape, scale, bound, pieces=(), kind=jnp.bfloat16):
    drawn = jax.random.normal(own_key, shape, jnp.float32) * scale
    if len(pieces) > 0:
        drawn = block_scale(own_key, shape, pieces, -0.22, 0.18) * drawn
    return jnp.clip(drawn, min=-bound, max=bound).astype(kind)


def setup_inputs(seed: int = 0) -> dict:
    seeds = jax.random.split(jax.random.key(seed), 7)
    return {
        "query": draw_query(jax.random.fold_in(seeds[6], 71), 0),
        "keys": draw_keys(jax.random.fold_in(seeds[6], 71), 0),
        "values": scatter_about(seeds[2], (TOKENS, HEADS * HEAD_DIM), 1.0, 6.0, ((0, 32), (1, 8))),
        "image_ids": jnp.searchsorted(jnp.cumsum(ragged_sizes(seeds[3], N_CTX, TOKENS, IMG_MAX, 2)), jnp.arange(TOKENS), side="right").astype(jnp.int32),
        "out_weight": scatter_about(seeds[4], (HEADS * HEAD_DIM, D), (HEADS * HEAD_DIM) ** -0.5, 0.109375, ((0, 8),)),
        "cotangent": scatter_about(seeds[5], (TOKENS, D), 1.0, 6.0, ((0, 32), (1, 8))),
    }


def split_heads(x):
    return x.reshape(x.shape[0], HEADS, HEAD_DIM).astype(jnp.float32)


def round_keep(x):
    return lax.optimization_barrier(x.astype(jnp.bfloat16)).astype(jnp.float32)


def reference(query, keys, values, image_ids, out_weight, cotangent):
    scale = HEAD_DIM ** -0.5
    width = TOK_DEV + 2 * IMG_MAX
    blocks = TOKENS // TOK_DEV

    def spread(x):
        return jnp.pad(x, ((IMG_MAX, IMG_MAX), (0, 0)))

    ids_wide = jnp.pad(image_ids, (IMG_MAX, IMG_MAX), constant_values=-1)

    def window(arr, block, axis=0):
        return lax.dynamic_slice_in_dim(arr, (block * TOK_DEV).astype(jnp.int32), width, axis)

    def own(arr, block, axis=0):
        return lax.dynamic_slice_in_dim(arr, (block * TOK_DEV).astype(jnp.int32), TOK_DEV, axis)

    keys_wide = spread(keys)
    values_wide = spread(values)

    def forward_block(block):
        q_b = split_heads(own(query, block))
        k_w = split_heads(window(keys_wide, block))
        v_w = split_heads(window(values_wide, block))
        mask = own(image_ids, block)[:, None] == window(ids_wide, block)[None, :]
        scores = jnp.einsum('qhe,khe->hqk', q_b, k_w) * scale
        scores = jnp.where(mask[None], scores, -jnp.inf)
        top = jnp.max(scores, axis=2, keepdims=True)
        lse = top + jnp.log(jnp.sum(jnp.exp(scores - top), axis=2, keepdims=True))
        probs = round_keep(jnp.exp(scores - lse))
        out = jnp.einsum('hqk,khe->qhe', probs, v_w)
        return out.reshape(TOK_DEV, HEADS * HEAD_DIM).astype(jnp.bfloat16), lse[:, :, 0]

    attended, lse = lax.map(forward_block, jnp.arange(blocks, dtype=jnp.int32))
    attended = attended.reshape(TOKENS, HEADS * HEAD_DIM)
    lse = jnp.transpose(lse, (1, 0, 2)).reshape(HEADS, TOKENS)

    mixed = jnp.dot(attended, out_weight, preferred_element_type=jnp.float32).astype(jnp.bfloat16)
    d_attended = lax.dot_general(cotangent, out_weight, (((1,), (1,)), ((), ())), preferred_element_type=jnp.float32).astype(jnp.bfloat16)
    grad_weight = lax.dot_general(attended, cotangent, (((0,), (0,)), ((), ())), preferred_element_type=jnp.float32).astype(jnp.bfloat16)
    delta = jnp.sum(split_heads(d_attended) * split_heads(attended), axis=2).T

    query_wide = spread(query)
    grads_wide = spread(d_attended)
    lse_wide = jnp.pad(lse, ((0, 0), (IMG_MAX, IMG_MAX)))
    delta_wide = jnp.pad(delta, ((0, 0), (IMG_MAX, IMG_MAX)))

    def query_block(block):
        q_b = split_heads(own(query, block))
        g_b = split_heads(own(d_attended, block))
        k_w = split_heads(window(keys_wide, block))
        v_w = split_heads(window(values_wide, block))
        lse_b = own(lse, block, 1)
        delta_b = own(delta, block, 1)
        mask = own(image_ids, block)[:, None] == window(ids_wide, block)[None, :]
        scores = jnp.einsum('qhe,khe->hqk', q_b, k_w) * scale
        scores = jnp.where(mask[None], scores, -jnp.inf)
        weight = jnp.exp(scores - lse_b[:, :, None])
        dots = jnp.einsum('qhe,khe->hqk', g_b, v_w)
        dscores = round_keep(weight * (dots - delta_b[:, :, None]))
        grad = jnp.einsum('hqk,khe->qhe', dscores, k_w) * scale
        return grad.reshape(TOK_DEV, HEADS * HEAD_DIM).astype(jnp.bfloat16)

    def key_block(block):
        k_b = split_heads(own(keys, block))
        v_b = split_heads(own(values, block))
        q_w = split_heads(window(query_wide, block))
        g_w = split_heads(window(grads_wide, block))
        lse_w = window(lse_wide, block, 1)
        delta_w = window(delta_wide, block, 1)
        mask = window(ids_wide, block)[:, None] == own(image_ids, block)[None, :]
        scores = jnp.einsum('qhe,khe->hqk', q_w, k_b) * scale
        scores = jnp.where(mask[None], scores, -jnp.inf)
        weight = jnp.exp(scores - lse_w[:, :, None])
        probs = round_keep(weight)
        grad_v = jnp.einsum('hqk,qhe->khe', probs, g_w)
        dots = jnp.einsum('qhe,khe->hqk', g_w, v_b)
        dscores = round_keep(weight * (dots - delta_w[:, :, None]))
        grad_k = jnp.einsum('hqk,qhe->khe', dscores, q_w) * scale
        return (grad_k.reshape(TOK_DEV, HEADS * HEAD_DIM).astype(jnp.bfloat16),
                grad_v.reshape(TOK_DEV, HEADS * HEAD_DIM).astype(jnp.bfloat16))

    grad_query = lax.map(query_block, jnp.arange(blocks, dtype=jnp.int32)).reshape(TOKENS, HEADS * HEAD_DIM)
    grad_keys, grad_values = lax.map(key_block, jnp.arange(blocks, dtype=jnp.int32))
    grad_keys = grad_keys.reshape(TOKENS, HEADS * HEAD_DIM)
    grad_values = grad_values.reshape(TOKENS, HEADS * HEAD_DIM)
    return (mixed, grad_query, grad_keys, grad_values, grad_weight)
```

```python
import functools

import jax
import jax.numpy as jnp
from jax import lax
from jax.experimental import pallas as pl
from jax.experimental.pallas import tpu as pltpu
from jax.sharding import PartitionSpec as P

HEAD = 128
ROWS = 512
COLS = 384
HEADS_DEV = COLS // HEAD
TP = 8
FEATURES = TP * COLS
WINDOW = 5
OWN = 2
CHUNK = 256
KEY_CHUNKS = WINDOW * ROWS // CHUNK
PIECE_ROWS = 48
PIECE_COLS = 768
NEG = -1e30
SCALE = HEAD ** -0.5
EXP2_SCALE = SCALE * 1.4426950408889634
F32 = jnp.float32
BF16 = jnp.bfloat16
MESH = pl.DeviceIdType.MESH
VMEM = pl.BlockSpec(memory_space=pltpu.VMEM)
SMEM = pl.BlockSpec(memory_space=pltpu.SMEM)
LIMIT = 56 * 1024 * 1024


class Links:
    def __init__(self, send_sem, recv_sem):
        self.send_sem, self.recv_sem = send_sem, recv_sem
        self.sent = []

    def _copy(self, src, dst, role, where):
        return pltpu.make_async_remote_copy(
            src_ref=src,
            dst_ref=dst,
            send_sem=self.send_sem.at[role],
            recv_sem=self.recv_sem.at[role],
            device_id=where,
            device_id_type=MESH,
        )

    def send(self, src, dst, role, where):
        copy = self._copy(src, dst, role, where)
        copy.start()
        self.sent.append(copy)

    def arrive(self, dst, role, where):
        self._copy(dst, dst, role, where).wait_recv()

    def finish(self):
        for copy in self.sent:
            copy.wait_send()


def greet(peers):
    barrier = pltpu.get_barrier_semaphore()
    for where in peers:
        pl.semaphore_signal(barrier, inc=1, device_id=where, device_id_type=MESH)
    pl.semaphore_wait(barrier, len(peers))


def ctx_ring(place, step):
    return {"ctx": lax.rem(place + step + 32, 32)}


def columns(index):
    return pl.ds(pl.multiple_of(index * COLS, COLS), COLS)


def gather_kernel(
    ids_ref, k_ref, v_ref, cot_ref, w_ref,
    ids_all, k_all, v_all, cot_all, dat_ref,
    acc, send_sem, recv_sem,
):
    place = lax.axis_index("ctx")
    part = lax.axis_index("tp")
    core = lax.rem(place, 2)
    high = lax.rem(part, 2)
    after, before = ctx_ring(place, 2), ctx_ring(place, -2)
    sibling = {"ctx": place + 1 - 2 * core}
    up, down = lax.rem(part + 2, TP), lax.rem(part + 6, TP)
    over = part + 1 - 2 * high
    across = lax.rem(part + 4, TP)
    y_up, y_down, far = {"tp": up}, {"tp": down}, {"tp": over}
    greet([after, before, sibling, y_up, y_down, far])
    links = Links(send_sem, recv_sem)

    links.send(cot_ref, cot_all.at[part], 12, far)
    links.send(cot_ref, cot_all.at[part], 13, y_up)
    links.send(cot_ref, cot_all.at[part], 14, y_down)
    arrays = ((ids_ref, ids_all), (k_ref, k_all), (v_ref, v_all))
    for n, (own, window) in enumerate(arrays):
        links.send(own, window.at[0], 4 * n, after)
        links.send(own, window.at[4], 4 * n + 1, before)
        links.send(own, window.at[1 + 2 * core], 4 * n + 2, sibling)
    for own, window in arrays:
        window[OWN] = own[...]
    cot_all[part] = cot_ref[...]

    def project(block, first=False):
        term = lax.dot_general(
            cot_all[block],
            w_ref[:, columns(block)],
            (((1,), (1,)), ((), ())),
            preferred_element_type=F32,
        )
        if first:
            acc[...] = term
        else:
            acc[...] += term

    def relay(n):
        window = arrays[n][1]
        links.arrive(window.at[0], 4 * n, before)
        links.arrive(window.at[4], 4 * n + 1, after)
        links.send(
            window.at[4 * (1 - core)], window.at[3 - 2 * core], 4 * n + 3, sibling
        )

    def forward(low_block, high_block, low_role, high_role, role):
        links.arrive(cot_all.at[low_block], low_role, y_down)
        links.send(
            cot_all.at[low_block, pl.ds(0, ROWS // 2)],
            cot_all.at[low_block, pl.ds(0, ROWS // 2)],
            role,
            y_up,
        )
        links.arrive(cot_all.at[high_block], high_role, y_up)
        links.send(
            cot_all.at[high_block, pl.ds(ROWS // 2, ROWS // 2)],
            cot_all.at[high_block, pl.ds(ROWS // 2, ROWS // 2)],
            role + 1,
            y_down,
        )

    def halves(block, role):
        links.arrive(cot_all.at[block, pl.ds(0, ROWS // 2)], role, y_down)
        links.arrive(cot_all.at[block, pl.ds(ROWS // 2, ROWS // 2)], role + 1, y_up)

    project(part, first=True)
    forward(down, up, 13, 14, 15)
    project(down)
    project(up)
    links.arrive(cot_all.at[over], 12, far)
    links.send(cot_all.at[over], cot_all.at[over], 17, y_up)
    links.send(cot_all.at[over], cot_all.at[over], 18, y_down)
    project(over)
    relay(0)
    halves(across, 15)
    project(across)
    relay(1)
    down_over = down + 1 - 2 * high
    up_over = up + 1 - 2 * high
    across_over = across + 1 - 2 * high
    forward(down_over, up_over, 17, 18, 19)
    project(down_over)
    project(up_over)
    relay(2)
    halves(across_over, 19)
    project(across_over)
    dat_ref[...] = acc[...].astype(BF16)
    for n, (own, window) in enumerate(arrays):
        links.arrive(window.at[3 - 2 * core], 4 * n + 2, sibling)
        links.arrive(window.at[1 + 2 * core], 4 * n + 3, sibling)
    links.finish()


def gather(ids, keys, values, cotangent, weight):
    return pl.pallas_call(
        gather_kernel,
        out_shape=(
            jax.ShapeDtypeStruct((WINDOW, 2, CHUNK), jnp.int32),
            jax.ShapeDtypeStruct((WINDOW, ROWS, COLS), BF16),
            jax.ShapeDtypeStruct((WINDOW, ROWS, COLS), BF16),
            jax.ShapeDtypeStruct((TP, ROWS, COLS), BF16),
            jax.ShapeDtypeStruct((ROWS, COLS), BF16),
        ),
        in_specs=[VMEM] * 5,
        out_specs=(VMEM,) * 5,
        scratch_shapes=[
            pltpu.VMEM((ROWS, COLS), F32),
            pltpu.SemaphoreType.DMA((21,)),
            pltpu.SemaphoreType.DMA((21,)),
        ],
        compiler_params=pltpu.CompilerParams(
            collective_id=0, has_side_effects=True, vmem_limit_bytes=LIMIT
        ),
        name="gather",
    )(ids, keys, values, cotangent, weight)


def dot(a, b, contract):
    return lax.dot_general(a, b, ((contract[:1], contract[1:]), ((), ())), preferred_element_type=F32)


def local_kernel(
    ids_smem, ids_col, ids_row, q_ref, k_ref, v_ref, dat_ref, cot_ref, w_ref,
    mixed_ref, wpart_ref, dq_ref, dkv_ref, own_ref,
    kept, out_acc, dq_acc, dk_acc, dv_acc, att,
):
    dk_acc[...] = jnp.zeros_like(dk_acc)
    dv_acc[...] = jnp.zeros_like(dv_acc)
    for qc in range(ROWS // CHUNK):
        rows = pl.ds(qc * CHUNK, CHUNK)
        q_first, q_last = ids_smem[OWN, qc, 0], ids_smem[OWN, qc, CHUNK - 1]
        lo, hi = jnp.int32(KEY_CHUNKS), jnp.int32(0)
        for kc in range(KEY_CHUNKS):
            s, r = kc // 2, kc % 2
            meets = (ids_smem[s, r, CHUNK - 1] >= q_first) & (ids_smem[s, r, 0] <= q_last)
            lo = jnp.minimum(lo, jnp.where(meets, kc, KEY_CHUNKS))
            hi = jnp.maximum(hi, jnp.where(meets, kc + 1, 0))
        q_ids = jnp.concatenate([ids_col[rows, :]] * (CHUNK // 128), axis=1)
        for h in range(HEADS_DEV):
            cols = pl.ds(h * HEAD, HEAD)
            q = q_ref[rows, cols]
            g = dat_ref[rows, cols]

            def keys_at(kc):
                return pl.ds(pl.multiple_of(kc * CHUNK, CHUNK), CHUNK)

            def score(kc, top):
                s = dot(q, k_ref[keys_at(kc), cols], (1, 1))
                k_ids = ids_row[lax.div(kc, 2), pl.ds(lax.rem(kc, 2), 1), :]
                s = jnp.where(q_ids == k_ids, s, NEG)
                kept[kc] = s
                return jnp.maximum(top, jnp.maximum(s[:, :128], s[:, 128:]))

            top = lax.fori_loop(lo, hi, score, jnp.full((CHUNK, 128), NEG, F32))
            top = jnp.max(top, axis=1, keepdims=True) * EXP2_SCALE
            top = jnp.broadcast_to(top, (CHUNK, CHUNK))
            out_acc[...] = jnp.zeros_like(out_acc)

            def attend(kc, total):
                p = jnp.exp2(kept[kc] * EXP2_SCALE - top)
                kept[kc] = p
                out_acc[...] += dot(p.astype(BF16), v_ref[keys_at(kc), cols], (1, 0))
                return total + (p[:, :128] + p[:, 128:])

            total = lax.fori_loop(lo, hi, attend, jnp.zeros((CHUNK, 128), F32))
            inverse = 1.0 / jnp.sum(total, axis=1, keepdims=True)
            attended = (out_acc[...] * inverse).astype(BF16)
            att[rows, cols] = attended
            delta = jnp.sum(g.astype(F32) * attended.astype(F32), axis=1, keepdims=True)
            inverse = jnp.broadcast_to(inverse, (CHUNK, CHUNK))
            delta = jnp.broadcast_to(delta, (CHUNK, CHUNK))
            dq_acc[...] = jnp.zeros_like(dq_acc)

            def back(kc, carry):
                here = keys_at(kc)
                k = k_ref[here, cols]
                dots = dot(g, v_ref[here, cols], (1, 1))
                weight = kept[kc] * inverse
                dscores = (weight * (dots - delta)).astype(BF16)
                dv_acc[here, cols] += dot(weight.astype(BF16), g, (0, 0))
                dk_acc[here, cols] += dot(dscores, q, (0, 0))
                dq_acc[...] += dot(dscores, k, (1, 0))
                return carry

            lax.fori_loop(lo, hi, back, 0)
            dq_ref[rows, cols] = (dq_acc[...] * SCALE).astype(BF16)
    for block in range(TP):
        cols = pl.ds(block * COLS, COLS)
        mixed_ref[block] = dot(att[...], w_ref[:, cols], (1, 0)).astype(BF16)
        term = dot(att[...], cot_ref[block], (0, 0)).astype(BF16)
        half = pl.ds((block % 2) * COLS, COLS)
        for c in range(2):
            for z in range(4):
                first = c * 192 + z * PIECE_ROWS
                wpart_ref[c, block // 2, z, :, half] = term[first : first + PIECE_ROWS]
    for s in range(WINDOW):
        here = pl.ds(s * ROWS, ROWS)
        if s == OWN:
            own_ref[0] = dk_acc[here, :] * SCALE
            own_ref[1] = dv_acc[here, :]
        else:
            dkv_ref[s, 0] = (dk_acc[here, :] * SCALE).astype(BF16)
            dkv_ref[s, 1] = dv_acc[here, :].astype(BF16)


def local(ids_all, ids_col, query, k_all, v_all, d_att, cot_all, weight):
    flat = (WINDOW * ROWS, COLS)
    return pl.pallas_call(
        local_kernel,
        out_shape=(
            jax.ShapeDtypeStruct((TP, ROWS, COLS), BF16),
            jax.ShapeDtypeStruct((2, 4, 4, PIECE_ROWS, PIECE_COLS), BF16),
            jax.ShapeDtypeStruct((ROWS, COLS), BF16),
            jax.ShapeDtypeStruct((WINDOW, 2, ROWS, COLS), BF16),
            jax.ShapeDtypeStruct((2, ROWS, COLS), F32),
        ),
        in_specs=[SMEM] + [VMEM] * 8,
        out_specs=(VMEM,) * 5,
        scratch_shapes=[
            pltpu.VMEM((KEY_CHUNKS, CHUNK, CHUNK), F32),
            pltpu.VMEM((CHUNK, HEAD), F32),
            pltpu.VMEM((CHUNK, HEAD), F32),
            pltpu.VMEM(flat, F32),
            pltpu.VMEM(flat, F32),
            pltpu.VMEM((ROWS, COLS), BF16),
        ],
        compiler_params=pltpu.CompilerParams(vmem_limit_bytes=LIMIT),
        name="local",
    )(
        ids_all, ids_col, ids_all, query, k_all.reshape(flat), v_all.reshape(flat),
        d_att, cot_all, weight,
    )


def reduce_kernel(
    m_ref, w_ref, dkv_ref, own_ref,
    mixed_ref, gk_ref, gv_ref, gw_ref,
    dkv_in, dkv_out, m_hop, m_in, m_out, m_far,
    w_core, w_sum, w_hop, w_in, w_x, w_z, w_all,
    send_sem, recv_sem,
):
    place = lax.axis_index("ctx")
    part = lax.axis_index("tp")
    core = lax.rem(place, 2)
    z = lax.rem(lax.div(place, 2), 4)
    x = lax.div(place, 8)
    high = lax.rem(part, 2)
    after, before = ctx_ring(place, 2), ctx_ring(place, -2)
    sibling = {"ctx": place + 1 - 2 * core}
    x_up, x_down = ctx_ring(place, 8), ctx_ring(place, -8)
    z_to = [{"ctx": 8 * x + 2 * lax.rem(z + d, 4) + core} for d in (1, 2, 3)]
    z_from = [{"ctx": 8 * x + 2 * lax.rem(z + 4 - d, 4) + core} for d in (1, 2, 3)]
    up, down = lax.rem(part + 2, TP), lax.rem(part + 6, TP)
    over = part + 1 - 2 * high
    across = lax.rem(part + 4, TP)
    y_up, y_down, far = {"tp": up}, {"tp": down}, {"tp": over}
    greet([after, before, sibling, x_up, x_down, y_up, y_down, far] + z_to)
    links = Links(send_sem, recv_sem)
    low, top = pl.ds(0, ROWS // 2), pl.ds(ROWS // 2, ROWS // 2)
    z_low, z_top = pl.ds(0, 2), pl.ds(2, 2)
    flip = 1 - 2 * high

    links.send(dkv_ref.at[1 + 2 * core], dkv_in.at[1], 1, sibling)
    links.send(w_ref.at[1 - core], w_core, 4, sibling)
    links.send(dkv_ref.at[3 - 2 * core], dkv_in.at[0], 0, sibling)

    planes = ((1, flip), (0, 0))
    for n, add in planes:
        links.send(m_ref.at[across + add, low], m_hop.at[n, 0], 10 + 10 * n, y_up)
        links.send(m_ref.at[across + add, top], m_hop.at[n, 1], 11 + 10 * n, y_down)
    for n, add in planes:
        links.send(m_ref.at[up + add, top], m_in.at[n, 0, top], 12 + 10 * n, y_up)
        links.send(m_ref.at[down + add, low], m_in.at[n, 1, low], 13 + 10 * n, y_down)
    direct = 4 * core

    @pl.when(core == 0)
    def _():
        links._copy(dkv_ref.at[0], dkv_in.at[2], 2, before).start()

    @pl.when(core == 1)
    def _():
        links._copy(dkv_ref.at[4], dkv_in.at[3], 3, after).start()

    links.arrive(dkv_in.at[1], 1, sibling)
    summed = 4 - direct
    for n in range(2):
        dkv_out[n] = (dkv_ref[summed, n].astype(F32) + dkv_in[1, n].astype(F32)).astype(BF16)

    @pl.when(core == 0)
    def _():
        links._copy(dkv_out, dkv_in.at[3], 3, after).start()

    @pl.when(core == 1)
    def _():
        links._copy(dkv_out, dkv_in.at[2], 2, before).start()

    links.arrive(w_core, 4, sibling)

    def add_cores(i, carry):
        w_sum[i] = (w_ref[core, i].astype(F32) + w_core[i].astype(F32)).astype(BF16)
        return carry

    def quarter(step):
        return lax.rem(x + step, 4)

    lax.fori_loop(0, 4, add_cores, 0)
    links.send(w_sum.at[quarter(2), z_low], w_hop.at[0], 30, x_up)
    links.send(w_sum.at[quarter(2), z_top], w_hop.at[1], 31, x_down)
    links.send(w_sum.at[quarter(1), z_top], w_in.at[0, z_top], 32, x_up)
    links.send(w_sum.at[quarter(3), z_low], w_in.at[1, z_low], 33, x_down)

    for n, add in planes:
        links.arrive(m_hop.at[n, 0], 10 + 10 * n, y_down)
        m_out[n, 0] = (m_ref[up + add, low].astype(F32) + m_hop[n, 0].astype(F32)).astype(BF16)
        links.send(m_out.at[n, 0], m_in.at[n, 0, low], 14 + 10 * n, y_up)
        links.arrive(m_hop.at[n, 1], 11 + 10 * n, y_up)
        m_out[n, 1] = (m_ref[down + add, top].astype(F32) + m_hop[n, 1].astype(F32)).astype(BF16)
        links.send(m_out.at[n, 1], m_in.at[n, 1, top], 15 + 10 * n, y_down)

    links.arrive(w_hop.at[0], 30, x_down)
    w_hop[0] = (w_sum[quarter(1), z_low].astype(F32) + w_hop[0].astype(F32)).astype(BF16)
    links.send(w_hop.at[0], w_in.at[0, z_low], 34, x_up)
    links.arrive(w_hop.at[1], 31, x_up)
    w_hop[1] = (w_sum[quarter(3), z_top].astype(F32) + w_hop[1].astype(F32)).astype(BF16)
    links.send(w_hop.at[1], w_in.at[1, z_top], 35, x_down)
    links.arrive(w_in.at[0, z_top], 32, x_down)
    links.arrive(w_in.at[1, z_low], 33, x_up)
    links.arrive(w_in.at[0, z_low], 34, x_down)
    links.arrive(w_in.at[1, z_top], 35, x_up)

    def add_x(i, carry):
        w_x[i] = (
            w_sum[x, i].astype(F32) + w_in[0, i].astype(F32) + w_in[1, i].astype(F32)
        ).astype(BF16)
        return carry

    lax.fori_loop(0, 4, add_x, 0)
    for d in range(3):
        links.send(w_x.at[lax.rem(z + d + 1, 4)], w_z.at[d], 36 + d, z_to[d])

    def along_y(n, add):
        links.arrive(m_in.at[n, 0, top], 12 + 10 * n, y_down)
        links.arrive(m_in.at[n, 1, low], 13 + 10 * n, y_up)
        links.arrive(m_in.at[n, 0, low], 14 + 10 * n, y_down)
        links.arrive(m_in.at[n, 1, top], 15 + 10 * n, y_up)
        return m_ref[part + add].astype(F32) + m_in[n, 0].astype(F32) + m_in[n, 1].astype(F32)

    def total_z():
        for d in range(3):
            links.arrive(w_z.at[d], 36 + d, z_from[d])
        w_all[core, x, z] = (
            w_x[z].astype(F32)
            + w_z[0].astype(F32)
            + w_z[1].astype(F32)
            + w_z[2].astype(F32)
        ).astype(BF16)
        for d in range(3):
            links.send(w_all.at[core, x, z], w_all.at[core, x, z], 39 + d, z_to[d])

    total_z()
    m_far[0] = along_y(1, flip).astype(BF16)
    links.send(m_far.at[0], m_far.at[1], 16, far)

    for d in range(3):
        links.arrive(w_all.at[core, x, lax.rem(z + 3 - d, 4)], 39 + d, z_from[d])
    links.send(w_all.at[core, x], w_all.at[core, x], 42, x_up)
    links.send(w_all.at[core, x], w_all.at[core, x], 43, x_down)
    links.send(w_all.at[core, x], w_all.at[core, x], 46, sibling)
    below, above, opposite = quarter(3), quarter(1), quarter(2)
    links.arrive(w_all.at[core, below], 42, x_down)
    links.send(w_all.at[core, below, z_low], w_all.at[core, below, z_low], 44, x_up)
    links.arrive(w_all.at[core, above], 43, x_up)
    links.send(w_all.at[core, above, z_top], w_all.at[core, above, z_top], 45, x_down)
    links.send(w_all.at[core, below], w_all.at[core, below], 47, sibling)
    links.send(w_all.at[core, above], w_all.at[core, above], 48, sibling)

    m_in[0, 0] = along_y(0, 0).astype(BF16)
    links.arrive(dkv_in.at[0], 0, sibling)
    links.arrive(dkv_in.at[2], 2, after)
    links.arrive(dkv_in.at[3], 3, before)
    for n, out in enumerate((gk_ref, gv_ref)):
        out[...] = (
            own_ref[n]
            + dkv_in[0, n].astype(F32)
            + dkv_in[2, n].astype(F32)
            + dkv_in[3, n].astype(F32)
        ).astype(BF16)

    links.arrive(w_all.at[core, opposite, z_low], 44, x_down)
    links.arrive(w_all.at[core, opposite, z_top], 45, x_up)
    links.send(w_all.at[core, opposite], w_all.at[core, opposite], 49, sibling)
    links.arrive(m_far.at[1], 16, far)
    mixed_ref[...] = (m_in[0, 0].astype(F32) + m_far[1].astype(F32)).astype(BF16)
    other = 1 - core
    for role, block in ((46, x), (47, below), (48, above), (49, opposite)):
        links.arrive(w_all.at[other, block], role, sibling)
    for c in range(2):
        for i in range(4):
            for j in range(4):
                gw_ref[
                    pl.ds(c * 192 + j * PIECE_ROWS, PIECE_ROWS), pl.ds(i * PIECE_COLS, PIECE_COLS)
                ] = w_all[c, i, j]
    links._copy(dkv_out, dkv_in.at[2], 2, before).wait_send()
    links._copy(dkv_out, dkv_in.at[3], 3, after).wait_send()
    links.finish()


def reduce(m_part, w_part, dkv, own):
    block = (ROWS, COLS)
    return pl.pallas_call(
        reduce_kernel,
        out_shape=(
            jax.ShapeDtypeStruct(block, BF16),
            jax.ShapeDtypeStruct(block, BF16),
            jax.ShapeDtypeStruct(block, BF16),
            jax.ShapeDtypeStruct((COLS, FEATURES), BF16),
        ),
        in_specs=[VMEM] * 4,
        out_specs=(VMEM,) * 4,
        scratch_shapes=[
            pltpu.VMEM((4, 2, ROWS, COLS), BF16),
            pltpu.VMEM((2, ROWS, COLS), BF16),
            pltpu.VMEM((2, 2, ROWS // 2, COLS), BF16),
            pltpu.VMEM((2, 2, ROWS, COLS), BF16),
            pltpu.VMEM((2, 2, ROWS // 2, COLS), BF16),
            pltpu.VMEM((2, ROWS, COLS), BF16),
            pltpu.VMEM((4, 4, PIECE_ROWS, PIECE_COLS), BF16),
            pltpu.VMEM((4, 4, PIECE_ROWS, PIECE_COLS), BF16),
            pltpu.VMEM((2, 2, PIECE_ROWS, PIECE_COLS), BF16),
            pltpu.VMEM((2, 4, PIECE_ROWS, PIECE_COLS), BF16),
            pltpu.VMEM((4, PIECE_ROWS, PIECE_COLS), BF16),
            pltpu.VMEM((3, PIECE_ROWS, PIECE_COLS), BF16),
            pltpu.VMEM((2, 4, 4, PIECE_ROWS, PIECE_COLS), BF16),
            pltpu.SemaphoreType.DMA((50,)),
            pltpu.SemaphoreType.DMA((50,)),
        ],
        compiler_params=pltpu.CompilerParams(
            collective_id=1, has_side_effects=True, vmem_limit_bytes=LIMIT
        ),
        name="reduce",
    )(m_part, w_part, dkv, own)


def on_device(query, keys, values, image_ids, out_weight, cotangent):
    ids_col = jnp.broadcast_to(image_ids[:, None], (ROWS, 128))
    ids_all, k_all, v_all, cot_all, d_att = gather(
        image_ids.reshape(2, CHUNK), keys, values, cotangent, out_weight
    )
    m_part, w_part, grad_query, dkv, own = local(
        ids_all, ids_col, query, k_all, v_all, d_att, cot_all, out_weight
    )
    mixed, grad_keys, grad_values, grad_weight = reduce(m_part, w_part, dkv, own)
    return (mixed, grad_query, grad_keys, grad_values, grad_weight)


def solution(mesh):
    placed = (
        P("ctx", "tp"),
        P("ctx", "tp"),
        P("ctx", "tp"),
        P("ctx"),
        P("tp", None),
        P("ctx", "tp"),
    )
    return jax.shard_map(
        on_device,
        mesh=mesh,
        in_specs=placed,
        out_specs=(P("ctx", "tp"), P("ctx", "tp"), P("ctx", "tp"), P("ctx", "tp"), P("tp", None)),
        check_vma=False,
    )
```

```python
import functools

import jax
import jax.numpy as jnp
from jax import lax
from jax.experimental import pallas as pl
from jax.experimental.pallas import tpu as pltpu
from jax.sharding import PartitionSpec as P

HEAD = 128
ROWS = 512
COLS = 384
HEADS_DEV = COLS // HEAD
TP = 8
FEATURES = TP * COLS
WINDOW = 5
OWN = 2
CHUNK = 256
HALF = ROWS // 2
PIECE_ROWS = 48
PIECE_COLS = 768
NEG = -1e30
SCALE = HEAD ** -0.5
EXP2_SCALE = SCALE * 1.4426950408889634
F32 = jnp.float32
BF16 = jnp.bfloat16
MESH = pl.DeviceIdType.MESH
VMEM = pl.BlockSpec(memory_space=pltpu.VMEM)
ANY = pl.BlockSpec(memory_space=pl.ANY)
LIMIT = 60 * 1024 * 1024


class Links:
    def __init__(self, send_sem, recv_sem):
        self.send_sem, self.recv_sem = send_sem, recv_sem
        self.sent = []

    def _copy(self, src, dst, role, where):
        return pltpu.make_async_remote_copy(
            src_ref=src,
            dst_ref=dst,
            send_sem=self.send_sem.at[role],
            recv_sem=self.recv_sem.at[role],
            device_id=where,
            device_id_type=MESH,
        )

    def send(self, src, dst, role, where, keep=True):
        copy = self._copy(src, dst, role, where)
        copy.start()
        if keep:
            self.sent.append(copy)

    def arrive(self, dst, role, where):
        self._copy(dst, dst, role, where).wait_recv()

    def left(self, src, role, where):
        self._copy(src, src, role, where).wait_send()

    def finish(self):
        for copy in self.sent:
            copy.wait_send()


def greet(peers):
    barrier = pltpu.get_barrier_semaphore()
    for where in peers:
        pl.semaphore_signal(barrier, inc=1, device_id=where, device_id_type=MESH)
    pl.semaphore_wait(barrier, len(peers))


def ctx_ring(place, step):
    return {"ctx": lax.rem(place + step + 32, 32)}


def columns(index):
    return pl.ds(pl.multiple_of(index * COLS, COLS), COLS)


IDS, KV, COT, DKV, MIX, FAR, CORE, XR, ZR, ZG, XG, CG, ROLES = (
    0, 4, 16, 25, 37, 49, 50, 54, 60, 63, 66, 70, 74,
)


def dot(a, b, contract):
    return lax.dot_general(
        a, b, ((contract[:1], contract[1:]), ((), ())), preferred_element_type=F32
    )


def wide(x, times):
    return jnp.concatenate([x] * times, axis=1)


def head_columns(h):
    return pl.ds(pl.multiple_of(h * HEAD, HEAD), HEAD)


def sublayer_kernel(
    ids_ref, ids_col, q_ref, k_ref, v_ref, cot_ref, w_ref,
    mixed_ref, gq_ref, gk_ref, gv_ref, gw_ref,
    ids_all, kv_all, cot_all, d_att, d_acc,
    top_ref, total_ref, out_acc, lse_ref, delta_ref, dq_acc, att, att_t,
    dkv, own, dkv_in,
    m_ref, m_hop, m_in, m_out, m_far,
    w_part, w_core, w_sum, w_hop, w_in, w_x, w_z, w_all,
    send_sem, recv_sem,
):
    place = lax.axis_index("ctx")
    part = lax.axis_index("tp")
    core = lax.rem(place, 2)
    z = lax.rem(lax.div(place, 2), 4)
    x = lax.div(place, 8)
    high = lax.rem(part, 2)
    flip = 1 - 2 * high
    after, before = ctx_ring(place, 2), ctx_ring(place, -2)
    sibling = {"ctx": place + 1 - 2 * core}
    x_up, x_down = ctx_ring(place, 8), ctx_ring(place, -8)
    z_to = [{"ctx": 8 * x + 2 * lax.rem(z + d, 4) + core} for d in (1, 2, 3)]
    z_from = [{"ctx": 8 * x + 2 * lax.rem(z + 4 - d, 4) + core} for d in (1, 2, 3)]
    up, down = lax.rem(part + 2, TP), lax.rem(part + 6, TP)
    across = lax.rem(part + 4, TP)
    over = part + flip
    y_up, y_down, far = {"tp": up}, {"tp": down}, {"tp": over}
    low, top = pl.ds(0, HALF), pl.ds(HALF, HALF)
    z_low, z_top = pl.ds(0, 2), pl.ds(2, 2)
    sib_slot, relay_slot = 3 - 2 * core, 1 + 2 * core
    direct_slot, sum_slot = 4 * core, 4 - 4 * core
    direct_to = {"ctx": lax.rem(place + 30 + 4 * core, 32)}
    sum_to = {"ctx": lax.rem(place + 34 - 4 * core, 32)}

    kv_all[OWN, 0] = k_ref[...]
    kv_all[OWN, 1] = v_ref[...]
    greet([after, before, sibling, x_up, x_down, y_up, y_down, far] + z_to)
    links = Links(send_sem, recv_sem)

    links.send(cot_ref, cot_all.at[part], COT, far)
    links.send(cot_ref, cot_all.at[part], COT + 1, y_up)
    links.send(cot_ref, cot_all.at[part], COT + 2, y_down)
    links.send(ids_ref, ids_all.at[0], IDS, after)
    links.send(ids_ref, ids_all.at[4], IDS + 1, before)
    links.send(ids_ref, ids_all.at[relay_slot], IDS + 2, sibling)

    def send_heads(h, carry):
        mine = kv_all.at[OWN, :, :, head_columns(h)]
        role = KV + 4 * h
        links.send(mine, kv_all.at[0, :, :, head_columns(h)], role, after, False)
        links.send(mine, kv_all.at[4, :, :, head_columns(h)], role + 1, before, False)
        links.send(mine, kv_all.at[relay_slot, :, :, head_columns(h)], role + 2, sibling, False)
        return carry

    lax.fori_loop(0, HEADS_DEV, send_heads, 0)
    ids_all[OWN] = ids_ref[...]
    cot_all[part] = cot_ref[...]

    def project(block, first=False):
        term = dot(cot_all[block], w_ref[:, columns(block)], (1, 1))
        if first:
            d_acc[...] = term
        else:
            d_acc[...] += term

    def key_ids(slot):
        return jnp.concatenate([ids_all[slot, 0:1, :], ids_all[slot, 1:2, :]], axis=1)

    def scores(h, slot):
        cols = head_columns(h)
        s = dot(q_ref[:, cols], kv_all[slot, 0, :, cols], (1, 1)) * EXP2_SCALE
        return jnp.where(wide(ids_col[...], ROWS // 128) == key_ids(slot), s, NEG)

    def lanes(op, s):
        return functools.reduce(op, [s[:, n : n + 128] for n in range(0, ROWS, 128)])

    def attend(h, slot, first=False):
        s = scores(h, slot)
        peak = jnp.max(lanes(jnp.maximum, s), axis=1, keepdims=True)
        peak = jnp.broadcast_to(peak, (ROWS, 128))
        if not first:
            old = top_ref[h]
            peak = jnp.maximum(old, peak)
            fade = jnp.exp2(old - peak)
        p = jnp.exp2(s - wide(peak, ROWS // 128))
        part_total = lanes(jnp.add, p)
        term = dot(p.astype(BF16), kv_all[slot, 1, :, head_columns(h)], (1, 0))
        if not first:
            part_total += total_ref[h] * fade
            term += out_acc[h] * fade
        total_ref[h] = part_total
        out_acc[h] = term
        top_ref[h] = peak

    def settle(h):
        cols = head_columns(h)
        total = jnp.sum(total_ref[h], axis=1, keepdims=True)
        attended = out_acc[h] * (1.0 / total)
        att_t[cols, :] = jnp.transpose(attended).astype(BF16)
        attended = attended.astype(BF16)
        att[:, cols] = attended
        lse_ref[...] = top_ref[h] + jnp.broadcast_to(jnp.log2(total), (ROWS, 128))
        delta = jnp.sum(
            attended.astype(F32) * d_att[:, cols].astype(F32), axis=1, keepdims=True
        )
        delta_ref[...] = jnp.broadcast_to(delta, (ROWS, 128))

    def back(h, slot, first=False, last=False):
        cols = head_columns(h)
        q, g = q_ref[:, cols], d_att[:, cols]
        k, v = kv_all[slot, 0, :, cols], kv_all[slot, 1, :, cols]
        weight = jnp.exp2(scores(h, slot) - wide(lse_ref[...], ROWS // 128))
        dots = dot(g, v, (1, 1))
        dscores = (weight * (dots - wide(delta_ref[...], ROWS // 128))).astype(BF16)
        dk = dot(dscores, q, (0, 0)) * SCALE
        dv = dot(weight.astype(BF16), g, (0, 0))
        dq = dot(dscores, k, (1, 0))
        if not first:
            dq += dq_acc[...]
        if last:
            own[0, :, cols] = dk
            own[1, :, cols] = dv
            gq_ref[:, cols] = (dq * SCALE).astype(BF16)
        else:
            dkv[slot, 0, :, cols] = dk.astype(BF16)
            dkv[slot, 1, :, cols] = dv.astype(BF16)
            dq_acc[...] = dq

    def each_head(work):
        def step(h, carry):
            work(h)
            return carry

        lax.fori_loop(0, HEADS_DEV, step, 0)

    def pass_on(low_block, high_block, low_role, high_role, role):
        links.arrive(cot_all.at[low_block], low_role, y_down)
        links.send(cot_all.at[low_block, low], cot_all.at[low_block, low], role, y_up, False)
        links.arrive(cot_all.at[high_block], high_role, y_up)
        links.send(
            cot_all.at[high_block, top], cot_all.at[high_block, top], role + 1, y_down, False
        )

    def halves(block, role):
        links.arrive(cot_all.at[block, low], role, y_down)
        links.arrive(cot_all.at[block, top], role + 1, y_up)

    project(part, first=True)
    each_head(lambda h: attend(h, OWN, first=True))
    pass_on(down, up, COT + 1, COT + 2, COT + 3)
    project(down)
    project(up)
    links.arrive(ids_all.at[0], IDS, before)
    links.arrive(ids_all.at[4], IDS + 1, after)
    links.send(ids_all.at[sum_slot], ids_all.at[sib_slot], IDS + 3, sibling)
    links.arrive(cot_all.at[over], COT, far)
    links.send(cot_all.at[over], cot_all.at[over], COT + 5, y_up)
    links.send(cot_all.at[over], cot_all.at[over], COT + 6, y_down)
    project(over)
    links.arrive(ids_all.at[sib_slot], IDS + 2, sibling)

    def attend_sibling(h):
        links.arrive(kv_all.at[sib_slot, :, :, head_columns(h)], KV + 4 * h + 2, sibling)
        attend(h, sib_slot)

    each_head(attend_sibling)
    halves(across, COT + 3)
    project(across)
    links.arrive(ids_all.at[relay_slot], IDS + 3, sibling)

    def rest_of_cotangent():
        down_over, up_over, across_over = down + flip, up + flip, across + flip
        pass_on(down_over, up_over, COT + 5, COT + 6, COT + 7)
        project(down_over)
        project(up_over)
        halves(across_over, COT + 7)
        project(across_over)
        d_att[...] = d_acc[...].astype(BF16)

    planes = ((1, flip), (0, 0))

    def share_heads():
        def mix(block):
            m_ref[block] = dot(att[...], w_ref[:, columns(block)], (1, 0)).astype(BF16)

        for n, add in planes:
            mix(across + add)
            role = MIX + 6 * n
            links.send(m_ref.at[across + add, low], m_hop.at[n, 0], role, y_up, False)
            links.send(m_ref.at[across + add, top], m_hop.at[n, 1], role + 1, y_down, False)

        def quarter_weight(n, carry):
            for side in range(2):
                term = dot(att_t[...], cot_all[2 * n + side], (1, 0)).astype(BF16)
                side_cols = pl.ds(side * COLS, COLS)
                for c in range(2):
                    for j in range(4):
                        first = c * 192 + j * PIECE_ROWS
                        w_part[c, n, j, :, side_cols] = term[first : first + PIECE_ROWS]
            links.send(w_part.at[1 - core, n], w_core.at[n], CORE + n, sibling, False)
            return carry

        lax.fori_loop(0, 4, quarter_weight, 0)
        for n, add in planes:
            mix(up + add)
            mix(down + add)
            role = MIX + 6 * n
            links.send(m_ref.at[up + add, top], m_in.at[n, 0, top], role + 2, y_up, False)
            links.send(m_ref.at[down + add, low], m_in.at[n, 1, low], role + 3, y_down, False)
        for n, add in planes:
            mix(part + add)

    def per_head(h):
        cols = head_columns(h)
        role = KV + 4 * h
        links.arrive(kv_all.at[0, :, :, cols], role, before)
        links.arrive(kv_all.at[4, :, :, cols], role + 1, after)
        links.send(
            kv_all.at[sum_slot, :, :, cols], kv_all.at[sib_slot, :, :, cols], role + 3, sibling,
            False,
        )
        attend(h, 0)
        attend(h, 4)
        pl.when(h == 0)(rest_of_cotangent)
        links.arrive(kv_all.at[relay_slot, :, :, cols], role + 3, sibling)
        attend(h, relay_slot)
        settle(h)
        pl.when(h == HEADS_DEV - 1)(share_heads)
        role = DKV + 4 * h
        back(h, relay_slot, first=True)
        links.send(
            dkv.at[relay_slot, :, :, cols], dkv_in.at[1, :, :, cols], role + 1, sibling, False
        )
        back(h, direct_slot)
        links.send(
            dkv.at[direct_slot, :, :, cols], dkv_in.at[2 + core, :, :, cols], role + 2 + core,
            direct_to, False,
        )
        back(h, sum_slot)
        links.arrive(dkv_in.at[1, :, :, cols], role + 1, sibling)
        for n in range(2):
            dkv[sum_slot, n, :, cols] = (
                dkv[sum_slot, n, :, cols].astype(F32) + dkv_in[1, n, :, cols].astype(F32)
            ).astype(BF16)
        links.send(
            dkv.at[sum_slot, :, :, cols], dkv_in.at[3 - core, :, :, cols], role + 3 - core,
            sum_to, False,
        )
        back(h, sib_slot)
        links.send(dkv.at[sib_slot, :, :, cols], dkv_in.at[0, :, :, cols], role, sibling, False)
        back(h, OWN, last=True)

    each_head(per_head)

    def quarter(step):
        return lax.rem(x + step, 4)

    def add_cores(i, carry):
        links.arrive(w_core.at[i], CORE + i, sibling)
        w_sum[i] = (w_part[core, i].astype(F32) + w_core[i].astype(F32)).astype(BF16)
        return carry

    lax.fori_loop(0, 4, add_cores, 0)
    links.send(w_sum.at[quarter(2), z_low], w_hop.at[0], XR, x_up)
    links.send(w_sum.at[quarter(2), z_top], w_hop.at[1], XR + 1, x_down)
    links.send(w_sum.at[quarter(1), z_top], w_in.at[0, z_top], XR + 2, x_up)
    links.send(w_sum.at[quarter(3), z_low], w_in.at[1, z_low], XR + 3, x_down)

    for n, add in planes:
        role = MIX + 6 * n
        links.arrive(m_hop.at[n, 0], role, y_down)
        m_out[n, 0] = (m_ref[up + add, low].astype(F32) + m_hop[n, 0].astype(F32)).astype(BF16)
        links.send(m_out.at[n, 0], m_in.at[n, 0, low], role + 4, y_up)
        links.arrive(m_hop.at[n, 1], role + 1, y_up)
        m_out[n, 1] = (m_ref[down + add, top].astype(F32) + m_hop[n, 1].astype(F32)).astype(BF16)
        links.send(m_out.at[n, 1], m_in.at[n, 1, top], role + 5, y_down)

    links.arrive(w_hop.at[0], XR, x_down)
    w_hop[0] = (w_sum[quarter(1), z_low].astype(F32) + w_hop[0].astype(F32)).astype(BF16)
    links.send(w_hop.at[0], w_in.at[0, z_low], XR + 4, x_up)
    links.arrive(w_hop.at[1], XR + 1, x_up)
    w_hop[1] = (w_sum[quarter(3), z_top].astype(F32) + w_hop[1].astype(F32)).astype(BF16)
    links.send(w_hop.at[1], w_in.at[1, z_top], XR + 5, x_down)
    links.arrive(w_in.at[0, z_top], XR + 2, x_down)
    links.arrive(w_in.at[1, z_low], XR + 3, x_up)
    links.arrive(w_in.at[0, z_low], XR + 4, x_down)
    links.arrive(w_in.at[1, z_top], XR + 5, x_up)

    def add_x(i, carry):
        w_x[i] = (
            w_sum[x, i].astype(F32) + w_in[0, i].astype(F32) + w_in[1, i].astype(F32)
        ).astype(BF16)
        return carry

    lax.fori_loop(0, 4, add_x, 0)
    for d in range(3):
        links.send(w_x.at[lax.rem(z + d + 1, 4)], w_z.at[d], ZR + d, z_to[d])

    def along_y(n, add):
        role = MIX + 6 * n
        links.arrive(m_in.at[n, 0, top], role + 2, y_down)
        links.arrive(m_in.at[n, 1, low], role + 3, y_up)
        links.arrive(m_in.at[n, 0, low], role + 4, y_down)
        links.arrive(m_in.at[n, 1, top], role + 5, y_up)
        return m_ref[part + add].astype(F32) + m_in[n, 0].astype(F32) + m_in[n, 1].astype(F32)

    for d in range(3):
        links.arrive(w_z.at[d], ZR + d, z_from[d])
    w_all[core, x, z] = (
        w_x[z].astype(F32) + w_z[0].astype(F32) + w_z[1].astype(F32) + w_z[2].astype(F32)
    ).astype(BF16)
    for d in range(3):
        links.send(w_all.at[core, x, z], w_all.at[core, x, z], ZG + d, z_to[d])

    m_far[0] = along_y(1, flip).astype(BF16)
    links.send(m_far.at[0], m_far.at[1], FAR, far)

    for d in range(3):
        links.arrive(w_all.at[core, x, lax.rem(z + 3 - d, 4)], ZG + d, z_from[d])
    links.send(w_all.at[core, x], w_all.at[core, x], XG, x_up)
    links.send(w_all.at[core, x], w_all.at[core, x], XG + 1, x_down)
    links.send(w_all.at[core, x], w_all.at[core, x], CG, sibling)
    below, above, opposite = quarter(3), quarter(1), quarter(2)
    links.arrive(w_all.at[core, below], XG, x_down)
    links.send(w_all.at[core, below, z_low], w_all.at[core, below, z_low], XG + 2, x_up)
    links.arrive(w_all.at[core, above], XG + 1, x_up)
    links.send(w_all.at[core, above, z_top], w_all.at[core, above, z_top], XG + 3, x_down)
    links.send(w_all.at[core, below], w_all.at[core, below], CG + 1, sibling)
    links.send(w_all.at[core, above], w_all.at[core, above], CG + 2, sibling)

    m_in[0, 0] = along_y(0, 0).astype(BF16)

    def add_keys(h):
        cols = head_columns(h)
        role = DKV + 4 * h
        links.arrive(dkv_in.at[0, :, :, cols], role, sibling)
        links.arrive(dkv_in.at[2, :, :, cols], role + 2, after)
        links.arrive(dkv_in.at[3, :, :, cols], role + 3, before)
        for n, out in enumerate((gk_ref, gv_ref)):
            out[:, cols] = (
                own[n, :, cols]
                + dkv_in[0, n, :, cols].astype(F32)
                + dkv_in[2, n, :, cols].astype(F32)
                + dkv_in[3, n, :, cols].astype(F32)
            ).astype(BF16)

    each_head(add_keys)
    links.arrive(w_all.at[core, opposite, z_low], XG + 2, x_down)
    links.arrive(w_all.at[core, opposite, z_top], XG + 3, x_up)
    links.send(w_all.at[core, opposite], w_all.at[core, opposite], CG + 3, sibling)
    links.arrive(m_far.at[1], FAR, far)
    mixed_ref[...] = (m_in[0, 0].astype(F32) + m_far[1].astype(F32)).astype(BF16)
    other = 1 - core
    for role, block in ((CG, x), (CG + 1, below), (CG + 2, above), (CG + 3, opposite)):
        links.arrive(w_all.at[other, block], role, sibling)
    for c in range(2):
        for i in range(4):
            for j in range(4):
                gw_ref[
                    pl.ds(c * 192 + j * PIECE_ROWS, PIECE_ROWS), pl.ds(i * PIECE_COLS, PIECE_COLS)
                ] = w_all[c, i, j]

    def heads_left(h):
        cols = head_columns(h)
        for n in range(4):
            links.left(kv_all.at[OWN, :, :, cols], KV + 4 * h + n, sibling)
            links.left(dkv.at[OWN, :, :, cols], DKV + 4 * h + n, sibling)

    each_head(heads_left)
    for n in range(2):
        for k in (0, 1, 2, 3):
            links.left(m_hop.at[n, 0], MIX + 6 * n + k, y_up)
    for n in range(4):
        links.left(w_core.at[n], CORE + n, sibling)
    for role in (3, 4, 7, 8):
        links.left(cot_all.at[0, low], COT + role, y_up)
    links.finish()


def sublayer(ids, ids_col, query, keys, values, cotangent, weight):
    block = (ROWS, COLS)
    bf16 = lambda *shape: pltpu.VMEM(shape, BF16)
    f32 = lambda *shape: pltpu.VMEM(shape, F32)
    heads = (HEADS_DEV, ROWS, HEAD)
    piece = (PIECE_ROWS, PIECE_COLS)
    return pl.pallas_call(
        sublayer_kernel,
        out_shape=tuple([jax.ShapeDtypeStruct(block, BF16)] * 4)
        + (jax.ShapeDtypeStruct((COLS, FEATURES), BF16),),
        in_specs=[VMEM] * 7,
        out_specs=(VMEM,) * 5,
        scratch_shapes=[
            pltpu.VMEM((WINDOW, 2, CHUNK), jnp.int32),
            bf16(WINDOW, 2, *block),
            bf16(TP, *block),
            bf16(*block),
            f32(*block),
            f32(*heads),
            f32(*heads),
            f32(*heads),
            f32(ROWS, HEAD),
            f32(ROWS, HEAD),
            f32(ROWS, HEAD),
            bf16(*block),
            bf16(COLS, ROWS),
            bf16(WINDOW, 2, *block),
            f32(2, *block),
            bf16(4, 2, *block),
            bf16(TP, *block),
            bf16(2, 2, HALF, COLS),
            bf16(2, 2, *block),
            bf16(2, 2, HALF, COLS),
            bf16(2, *block),
            bf16(2, 4, 4, *piece),
            bf16(4, 4, *piece),
            bf16(4, 4, *piece),
            bf16(2, 2, *piece),
            bf16(2, 4, *piece),
            bf16(4, *piece),
            bf16(3, *piece),
            bf16(2, 4, 4, *piece),
            pltpu.SemaphoreType.DMA((ROLES,)),
            pltpu.SemaphoreType.DMA((ROLES,)),
        ],
        compiler_params=pltpu.CompilerParams(
            collective_id=0, has_side_effects=True, vmem_limit_bytes=LIMIT
        ),
        name="sublayer",
    )(ids, ids_col, query, keys, values, cotangent, weight)


def hand_over_kernel(*refs):
    count = len(refs) // 2
    for n in range(count):
        refs[count + n][...] = refs[n][...]


def hand_over(arrays):
    return pl.pallas_call(
        hand_over_kernel,
        out_shape=tuple(jax.ShapeDtypeStruct(a.shape, a.dtype) for a in arrays),
        in_specs=[VMEM] * len(arrays),
        out_specs=(VMEM,) * len(arrays),
        name="hand_over",
    )(*arrays)


def on_device(query, keys, values, image_ids, out_weight, cotangent):
    ids_col = jnp.broadcast_to(image_ids[:, None], (ROWS, 128))
    return hand_over(
        sublayer(
            image_ids.reshape(2, CHUNK), ids_col, query, keys, values, cotangent, out_weight
        )
    )


def solution(mesh):
    placed = (
        P("ctx", "tp"),
        P("ctx", "tp"),
        P("ctx", "tp"),
        P("ctx"),
        P("tp", None),
        P("ctx", "tp"),
    )
    return jax.shard_map(
        on_device,
        mesh=mesh,
        in_specs=placed,
        out_specs=(P("ctx", "tp"), P("ctx", "tp"), P("ctx", "tp"), P("ctx", "tp"), P("tp", None)),
        check_vma=False,
    )
```

```python
import functools

import jax
import jax.numpy as jnp
from jax import lax
from jax.experimental import pallas as pl
from jax.experimental.pallas import tpu as pltpu
from jax.sharding import PartitionSpec as P

HEAD = 128
ROWS = 512
COLS = 384
HEADS_DEV = COLS // HEAD
TP = 8
FEATURES = TP * COLS
WINDOW = 5
OWN = 2
CHUNK = 256
HALF = ROWS // 2
PIECE_ROWS = 16
PIECE_COLS = 768
NEG = -1e30
SCALE = HEAD ** -0.5
EXP2_SCALE = SCALE * 1.4426950408889634
F32 = jnp.float32
BF16 = jnp.bfloat16
MESH = pl.DeviceIdType.MESH
VMEM = pl.BlockSpec(memory_space=pltpu.VMEM)
ANY = pl.BlockSpec(memory_space=pl.ANY)
LIMIT = 60 * 1024 * 1024


class Links:
    def __init__(self, send_sem, recv_sem):
        self.send_sem, self.recv_sem = send_sem, recv_sem
        self.sent = []

    def _copy(self, src, dst, role, where):
        return pltpu.make_async_remote_copy(
            src_ref=src,
            dst_ref=dst,
            send_sem=self.send_sem.at[role],
            recv_sem=self.recv_sem.at[role],
            device_id=where,
            device_id_type=MESH,
        )

    def send(self, src, dst, role, where, keep=True):
        copy = self._copy(src, dst, role, where)
        copy.start()
        if keep:
            self.sent.append(copy)

    def arrive(self, dst, role, where):
        self._copy(dst, dst, role, where).wait_recv()

    def left(self, src, role, where):
        self._copy(src, src, role, where).wait_send()

    def finish(self):
        for copy in self.sent:
            copy.wait_send()


def greet(peers):
    barrier = pltpu.get_barrier_semaphore()
    for where in peers:
        pl.semaphore_signal(barrier, inc=1, device_id=where, device_id_type=MESH)
    pl.semaphore_wait(barrier, len(peers))


def ctx_ring(place, step):
    return {"ctx": lax.rem(place + step + 32, 32)}


def columns(index):
    return pl.ds(pl.multiple_of(index * COLS, COLS), COLS)


IDS, KV, COT, DKV, MIX, FAR, SUM, ROLES = 0, 4, 16, 28, 40, 52, 53, 116
CORE, XR, ZR, ZG, XG, CG, SUM_ROLES = 0, 1, 7, 10, 13, 17, 21


def dot(a, b, contract):
    return lax.dot_general(
        a, b, ((contract[:1], contract[1:]), ((), ())), preferred_element_type=F32
    )


def wide(x, times):
    return jnp.concatenate([x] * times, axis=1)


def head_columns(h):
    return pl.ds(pl.multiple_of(h * HEAD, HEAD), HEAD)


def sublayer_kernel(
    ids_ref, q_ref, k_ref, v_ref, cot_ref, w_ref,
    mixed_ref, gq_ref, gk_ref, gv_ref, gw_ref,
    ids_all, ids_col, kv_all, cot_all, d_att, d_acc,
    top_ref, total_ref, out_acc, lse_ref, delta_ref, dq_acc, att, att_t,
    dkv, own, dkv_in,
    m_ref, m_hop, m_in, m_out, m_far,
    w_part, w_core, w_sum, w_hop, w_in, w_x, w_z,
    send_sem, recv_sem,
):
    place = lax.axis_index("ctx")
    part = lax.axis_index("tp")
    core = lax.rem(place, 2)
    z = lax.rem(lax.div(place, 2), 4)
    x = lax.div(place, 8)
    high = lax.rem(part, 2)
    flip = 1 - 2 * high
    after, before = ctx_ring(place, 2), ctx_ring(place, -2)
    sibling = {"ctx": place + 1 - 2 * core}
    x_up, x_down = ctx_ring(place, 8), ctx_ring(place, -8)
    z_to = [{"ctx": 8 * x + 2 * lax.rem(z + d, 4) + core} for d in (1, 2, 3)]
    z_from = [{"ctx": 8 * x + 2 * lax.rem(z + 4 - d, 4) + core} for d in (1, 2, 3)]
    up, down = lax.rem(part + 2, TP), lax.rem(part + 6, TP)
    across = lax.rem(part + 4, TP)
    over = part + flip
    y_up, y_down, far = {"tp": up}, {"tp": down}, {"tp": over}
    low, top = pl.ds(0, HALF), pl.ds(HALF, HALF)
    z_low, z_top = pl.ds(0, 2), pl.ds(2, 2)
    sib_slot, relay_slot = 3 - 2 * core, 1 + 2 * core
    direct_slot, sum_slot = 4 * core, 4 - 4 * core
    direct_to = {"ctx": lax.rem(place + 30 + 4 * core, 32)}
    sum_to = {"ctx": lax.rem(place + 34 - 4 * core, 32)}

    kv_all[OWN, 0] = k_ref[...]
    kv_all[OWN, 1] = v_ref[...]
    ids_all[OWN] = ids_ref[...].reshape(1, ROWS)
    greet([after, before, sibling, x_up, x_down, y_up, y_down, far] + z_to)
    links = Links(send_sem, recv_sem)

    links.send(cot_ref.at[low], cot_all.at[part, low], COT, far)
    links.send(cot_ref.at[top], cot_all.at[part, top], COT + 9, far)
    links.send(cot_ref, cot_all.at[part], COT + 1, y_up)
    links.send(cot_ref, cot_all.at[part], COT + 2, y_down)
    links.send(ids_all.at[OWN], ids_all.at[0], IDS, after)
    links.send(ids_all.at[OWN], ids_all.at[4], IDS + 1, before)
    links.send(ids_all.at[OWN], ids_all.at[relay_slot], IDS + 2, sibling)

    def send_heads(h):
        mine = kv_all.at[OWN, :, :, head_columns(h)]
        role = KV + 4 * h
        links.send(mine, kv_all.at[0, :, :, head_columns(h)], role, after, False)
        links.send(mine, kv_all.at[4, :, :, head_columns(h)], role + 1, before, False)
        links.send(mine, kv_all.at[relay_slot, :, :, head_columns(h)], role + 2, sibling, False)

    send_heads(0)
    for n in range(ROWS // 128):
        piece = jnp.broadcast_to(ids_all[OWN, :, pl.ds(n * 128, 128)], (128, 128))
        ids_col[pl.ds(n * 128, 128), :] = jnp.transpose(piece)
    cot_all[part] = cot_ref[...]

    def project(block, first=False):
        term = dot(cot_all[block], w_ref[:, columns(block)], (1, 1))
        if first:
            d_acc[...] = term
        else:
            d_acc[...] += term

    def key_ids(slot):
        return ids_all[slot]

    def scores(h, slot):
        cols = head_columns(h)
        s = dot(q_ref[:, cols], kv_all[slot, 0, :, cols], (1, 1)) * EXP2_SCALE
        return jnp.where(wide(ids_col[...], ROWS // 128) == key_ids(slot), s, NEG)

    def lanes(op, s):
        return functools.reduce(op, [s[:, n : n + 128] for n in range(0, ROWS, 128)])

    def attend(h, slot, first=False):
        s = scores(h, slot)
        peak = jnp.max(lanes(jnp.maximum, s), axis=1, keepdims=True)
        peak = jnp.broadcast_to(peak, (ROWS, 128))
        if not first:
            old = top_ref[h]
            peak = jnp.maximum(old, peak)
            fade = jnp.exp2(old - peak)
        p = jnp.exp2(s - wide(peak, ROWS // 128))
        part_total = lanes(jnp.add, p)
        term = dot(p.astype(BF16), kv_all[slot, 1, :, head_columns(h)], (1, 0))
        if not first:
            part_total += total_ref[h] * fade
            term += out_acc[h] * fade
        total_ref[h] = part_total
        out_acc[h] = term
        top_ref[h] = peak

    def settle(h):
        cols = head_columns(h)
        total = jnp.sum(total_ref[h], axis=1, keepdims=True)
        attended = out_acc[h] * (1.0 / total)
        att_t[cols, :] = jnp.transpose(attended).astype(BF16)
        attended = attended.astype(BF16)
        att[:, cols] = attended
        lse_ref[...] = top_ref[h] + jnp.broadcast_to(jnp.log2(total), (ROWS, 128))
        delta = jnp.sum(
            attended.astype(F32) * d_att[:, cols].astype(F32), axis=1, keepdims=True
        )
        delta_ref[...] = jnp.broadcast_to(delta, (ROWS, 128))

    def back(h, slot, first=False, last=False):
        cols = head_columns(h)
        q, g = q_ref[:, cols], d_att[:, cols]
        k, v = kv_all[slot, 0, :, cols], kv_all[slot, 1, :, cols]
        weight = jnp.exp2(scores(h, slot) - wide(lse_ref[...], ROWS // 128))
        dots = dot(g, v, (1, 1))
        dscores = (weight * (dots - wide(delta_ref[...], ROWS // 128))).astype(BF16)
        dk = dot(dscores, q, (0, 0)) * SCALE
        dv = dot(weight.astype(BF16), g, (0, 0))
        dq = dot(dscores, k, (1, 0))
        if not first:
            dq += dq_acc[...]
        if last:
            own[0, :, cols] = dk
            own[1, :, cols] = dv
            gq_ref[:, cols] = (dq * SCALE).astype(BF16)
        else:
            dkv[slot, 0, :, cols] = dk.astype(BF16)
            dkv[slot, 1, :, cols] = dv.astype(BF16)
            dq_acc[...] = dq

    def each_head(work):
        def step(h, carry):
            work(h)
            return carry

        lax.fori_loop(0, HEADS_DEV, step, 0)

    def send_half(block, half, role, where):
        links.send(cot_all.at[block, half], cot_all.at[block, half], role, where, False)

    def halves(block, role):
        links.arrive(cot_all.at[block, low], role, y_down)
        links.arrive(cot_all.at[block, top], role + 1, y_up)

    project(part, first=True)
    each_head(lambda h: attend(h, OWN, first=True))
    links.arrive(cot_all.at[down], COT + 1, y_down)
    send_half(down, low, COT + 3, y_up)
    links.arrive(cot_all.at[up], COT + 2, y_up)
    send_half(up, top, COT + 4, y_down)
    send_heads(1)
    project(down)
    project(up)
    links.arrive(ids_all.at[0], IDS, before)
    links.arrive(ids_all.at[4], IDS + 1, after)
    links.send(ids_all.at[sum_slot], ids_all.at[sib_slot], IDS + 3, sibling)
    links.arrive(cot_all.at[over, low], COT, far)
    send_half(over, low, COT + 5, y_up)
    send_half(over, low, COT + 6, y_down)
    links.arrive(cot_all.at[over, top], COT + 9, far)
    send_half(over, top, COT + 10, y_up)
    send_half(over, top, COT + 11, y_down)
    project(over)
    send_heads(2)
    links.arrive(ids_all.at[sib_slot], IDS + 2, sibling)

    def attend_sibling(h):
        links.arrive(kv_all.at[sib_slot, :, :, head_columns(h)], KV + 4 * h + 2, sibling)
        attend(h, sib_slot)

    each_head(attend_sibling)
    halves(across, COT + 3)
    project(across)
    links.arrive(ids_all.at[relay_slot], IDS + 3, sibling)

    down_over, up_over, across_over = down + flip, up + flip, across + flip
    links.arrive(cot_all.at[down_over, low], COT + 5, y_down)
    send_half(down_over, low, COT + 7, y_up)
    links.arrive(cot_all.at[up_over, top], COT + 11, y_up)
    send_half(up_over, top, COT + 8, y_down)

    def rest_of_cotangent():
        links.arrive(cot_all.at[down_over, top], COT + 10, y_down)
        links.arrive(cot_all.at[up_over, low], COT + 6, y_up)
        project(down_over)
        project(up_over)
        halves(across_over, COT + 7)
        project(across_over)
        d_att[...] = d_acc[...].astype(BF16)

    planes = (0, flip)

    def share_plane(n):
        add = planes[n]
        role = MIX + 6 * n

        def mix(block):
            m_ref[block] = dot(att[...], w_ref[:, columns(block)], (1, 0)).astype(BF16)

        mix(across + add)
        links.send(m_ref.at[across + add, low], m_hop.at[n, 0], role, y_up, False)
        links.send(m_ref.at[across + add, top], m_hop.at[n, 1], role + 1, y_down, False)
        mix(up + add)
        links.send(m_ref.at[up + add, top], m_in.at[n, 0, top], role + 2, y_up, False)
        mix(down + add)
        links.send(m_ref.at[down + add, low], m_in.at[n, 1, low], role + 3, y_down, False)
        mix(part + add)

    def plane_hops(n):
        add = planes[n]
        role = MIX + 6 * n
        links.arrive(m_hop.at[n, 0], role, y_down)
        m_out[n, 0] = add_up(m_ref[up + add, low], m_hop[n, 0])
        links.send(m_out.at[n, 0], m_in.at[n, 0, low], role + 4, y_up, False)
        links.arrive(m_hop.at[n, 1], role + 1, y_up)
        m_out[n, 1] = add_up(m_ref[down + add, top], m_hop[n, 1])
        links.send(m_out.at[n, 1], m_in.at[n, 1, top], role + 5, y_down, False)

    def quarter(step):
        return lax.rem(x + step, 4)

    below, above, opposite = quarter(3), quarter(1), quarter(2)

    def weight_rows(h):
        rows = head_columns(h)

        def two_blocks(n, carry):
            for side in range(2):
                term = dot(att_t[rows, :], cot_all[2 * n + side], (1, 0)).astype(BF16)
                side_cols = pl.ds(side * COLS, COLS)
                for c in range(2):
                    for j in range(4):
                        first = (4 * c + j) * PIECE_ROWS
                        w_part[h, c, n, j, :, side_cols] = term[first : first + PIECE_ROWS]
            return carry

        lax.fori_loop(0, 4, two_blocks, 0)
        links.send(
            w_part.at[h, 1 - core], w_core.at[h], SUM + SUM_ROLES * h + CORE, sibling, False
        )

    def out_rows(h, c, first, count):
        start = h * HEAD + c * (HEAD // 2) + first * PIECE_ROWS
        return pl.ds(pl.multiple_of(start, PIECE_ROWS), count * PIECE_ROWS)

    def out_cols(block):
        return pl.ds(pl.multiple_of(block * PIECE_COLS, PIECE_COLS), PIECE_COLS)

    def add_up(*terms):
        return sum(t.astype(F32) for t in terms).astype(BF16)

    def sum_cores(h):
        role = SUM + SUM_ROLES * h
        links.arrive(w_core.at[h], role + CORE, sibling)

        def add(i, carry):
            w_sum[h, i] = add_up(w_part[h, core, i], w_core[h, i])
            return carry

        lax.fori_loop(0, 4, add, 0)
        role += XR
        links.send(w_sum.at[h, opposite, z_low], w_hop.at[h, 0], role, x_up, False)
        links.send(w_sum.at[h, opposite, z_top], w_hop.at[h, 1], role + 1, x_down, False)
        links.send(w_sum.at[h, above, z_top], w_in.at[h, 0, z_top], role + 2, x_up, False)
        links.send(w_sum.at[h, below, z_low], w_in.at[h, 1, z_low], role + 3, x_down, False)

    def sum_hops(h):
        role = SUM + SUM_ROLES * h + XR
        links.arrive(w_hop.at[h, 0], role, x_down)
        w_hop[h, 0] = add_up(w_sum[h, above, z_low], w_hop[h, 0])
        links.send(w_hop.at[h, 0], w_in.at[h, 0, z_low], role + 4, x_up, False)
        links.arrive(w_hop.at[h, 1], role + 1, x_up)
        w_hop[h, 1] = add_up(w_sum[h, below, z_top], w_hop[h, 1])
        links.send(w_hop.at[h, 1], w_in.at[h, 1, z_top], role + 5, x_down, False)

    def sum_x(h):
        role = SUM + SUM_ROLES * h + XR
        links.arrive(w_in.at[h, 0, z_top], role + 2, x_down)
        links.arrive(w_in.at[h, 1, z_low], role + 3, x_up)
        links.arrive(w_in.at[h, 0, z_low], role + 4, x_down)
        links.arrive(w_in.at[h, 1, z_top], role + 5, x_up)
        w_x[h] = add_up(w_sum[h, x], w_in[h, 0], w_in[h, 1])
        role = SUM + SUM_ROLES * h + ZR
        for d in range(3):
            links.send(w_x.at[h, lax.rem(z + d + 1, 4)], w_z.at[h, d], role + d, z_to[d], False)

    def sum_z(h):
        role = SUM + SUM_ROLES * h + ZR
        for d in range(3):
            links.arrive(w_z.at[h, d], role + d, z_from[d])
        mine = gw_ref.at[out_rows(h, core, z, 1), out_cols(x)]
        mine[...] = add_up(w_x[h, z], w_z[h, 0], w_z[h, 1], w_z[h, 2])
        role = SUM + SUM_ROLES * h + ZG
        for d in range(3):
            links.send(mine, mine, role + d, z_to[d], False)

    def spread_x(h):
        role = SUM + SUM_ROLES * h
        for d in range(3):
            rows = out_rows(h, core, lax.rem(z + 3 - d, 4), 1)
            links.arrive(gw_ref.at[rows, out_cols(x)], role + ZG + d, z_from[d])
        mine = gw_ref.at[out_rows(h, core, 0, 4), out_cols(x)]
        links.send(mine, mine, role + XG, x_up, False)
        links.send(mine, mine, role + XG + 1, x_down, False)
        links.send(mine, mine, role + CG, sibling, False)

    def spread_on(h):
        role = SUM + SUM_ROLES * h
        for n, (block, back_from, on_to) in enumerate(((below, x_down, x_up), (above, x_up, x_down))):
            whole = gw_ref.at[out_rows(h, core, 0, 4), out_cols(block)]
            part_of = gw_ref.at[out_rows(h, core, 2 * n, 2), out_cols(block)]
            links.arrive(whole, role + XG + n, back_from)
            links.send(part_of, part_of, role + XG + 2 + n, on_to, False)
            links.send(whole, whole, role + CG + 1 + n, sibling, False)

    def spread_cores(h):
        role = SUM + SUM_ROLES * h
        for n, back_from in enumerate((x_down, x_up)):
            part_of = gw_ref.at[out_rows(h, core, 2 * n, 2), out_cols(opposite)]
            links.arrive(part_of, role + XG + 2 + n, back_from)
        whole = gw_ref.at[out_rows(h, core, 0, 4), out_cols(opposite)]
        links.send(whole, whole, role + CG + 3, sibling, False)

    def spread_done(h):
        role = SUM + SUM_ROLES * h + CG
        for n, block in enumerate((x, below, above, opposite)):
            links.arrive(gw_ref.at[out_rows(h, 1 - core, 0, 4), out_cols(block)], role + n, sibling)

    def sum_left(h):
        role = SUM + SUM_ROLES * h
        links.left(w_core.at[h], role + CORE, sibling)
        for n in range(6):
            links.left(w_hop.at[h, 0], role + XR + n, x_up)
        for n in range(3):
            links.left(w_z.at[h, n], role + ZR + n, z_to[n])
            links.left(w_z.at[h, n], role + ZG + n, z_to[n])
        whole = gw_ref.at[out_rows(h, core, 0, 4), out_cols(x)]
        half = gw_ref.at[out_rows(h, core, 0, 2), out_cols(x)]
        for n in range(2):
            links.left(whole, role + XG + n, x_up)
            links.left(half, role + XG + 2 + n, x_up)
        for n in range(4):
            links.left(whole, role + CG + n, sibling)

    final = HEADS_DEV - 1

    def per_head(h):
        def of_last(step):
            pl.when(h > 0)(lambda: step(h - 1))

        cols = head_columns(h)
        role = KV + 4 * h
        links.arrive(kv_all.at[0, :, :, cols], role, before)
        links.arrive(kv_all.at[4, :, :, cols], role + 1, after)
        links.send(
            kv_all.at[sum_slot, :, :, cols], kv_all.at[sib_slot, :, :, cols], role + 3, sibling,
            False,
        )
        attend(h, 0)
        attend(h, 4)
        pl.when(h == 0)(rest_of_cotangent)
        links.arrive(kv_all.at[relay_slot, :, :, cols], role + 3, sibling)
        attend(h, relay_slot)
        settle(h)
        pl.when(h == final)(lambda: share_plane(1))
        weight_rows(h)
        role = DKV + 4 * h
        back(h, relay_slot, first=True)
        links.send(
            dkv.at[relay_slot, :, :, cols], dkv_in.at[1, :, :, cols], role + 1, sibling, False
        )
        sum_cores(h)
        back(h, direct_slot)
        links.send(
            dkv.at[direct_slot, :, :, cols], dkv_in.at[2 + core, :, :, cols], role + 2 + core,
            direct_to, False,
        )
        of_last(sum_x)
        back(h, sum_slot)
        links.arrive(dkv_in.at[1, :, :, cols], role + 1, sibling)
        for n in range(2):
            dkv[sum_slot, n, :, cols] = add_up(
                dkv[sum_slot, n, :, cols], dkv_in[1, n, :, cols]
            )
        links.send(
            dkv.at[sum_slot, :, :, cols], dkv_in.at[3 - core, :, :, cols], role + 3 - core,
            sum_to, False,
        )
        back(h, sib_slot)
        links.send(dkv.at[sib_slot, :, :, cols], dkv_in.at[0, :, :, cols], role, sibling, False)

        @pl.when(h == final)
        def _():
            plane_hops(1)
            share_plane(0)

        sum_hops(h)
        back(h, OWN, last=True)

    each_head(per_head)

    def along_y(n):
        add = planes[n]
        role = MIX + 6 * n
        links.arrive(m_in.at[n, 0, top], role + 2, y_down)
        links.arrive(m_in.at[n, 1, low], role + 3, y_up)
        links.arrive(m_in.at[n, 0, low], role + 4, y_down)
        links.arrive(m_in.at[n, 1, top], role + 5, y_up)
        return add_up(m_ref[part + add], m_in[n, 0], m_in[n, 1])

    def add_keys(h):
        cols = head_columns(h)
        role = DKV + 4 * h
        links.arrive(dkv_in.at[0, :, :, cols], role, sibling)
        links.arrive(dkv_in.at[2, :, :, cols], role + 2, after)
        links.arrive(dkv_in.at[3, :, :, cols], role + 3, before)
        for n, out in enumerate((gk_ref, gv_ref)):
            out[:, cols] = add_up(
                own[n, :, cols], dkv_in[0, n, :, cols], dkv_in[2, n, :, cols],
                dkv_in[3, n, :, cols],
            )

    sum_x(final)
    sum_z(0)
    sum_z(1)
    plane_hops(0)
    spread_x(0)
    spread_x(1)
    sum_z(final)
    m_far[0] = along_y(1)
    links.send(m_far.at[0], m_far.at[1], FAR, far)
    spread_on(0)
    spread_on(1)
    spread_x(final)
    spread_cores(0)
    spread_cores(1)
    m_in[0, 0] = along_y(0)
    spread_on(final)
    each_head(add_keys)
    spread_cores(final)
    links.arrive(m_far.at[1], FAR, far)
    mixed_ref[...] = add_up(m_in[0, 0], m_far[1])
    each_head(spread_done)

    def heads_left(h):
        cols = head_columns(h)
        for n in range(4):
            links.left(kv_all.at[OWN, :, :, cols], KV + 4 * h + n, sibling)
            links.left(dkv.at[OWN, :, :, cols], DKV + 4 * h + n, sibling)
        sum_left(h)

    each_head(heads_left)
    for n in range(2):
        for k in range(6):
            links.left(m_hop.at[n, 0], MIX + 6 * n + k, y_up)
    for role in (3, 4, 5, 6, 7, 8, 10, 11):
        links.left(cot_all.at[0, low], COT + role, y_up)
    links.finish()


def sublayer(ids, query, keys, values, cotangent, weight):
    block = (ROWS, COLS)
    bf16 = lambda *shape: pltpu.VMEM(shape, BF16)
    f32 = lambda *shape: pltpu.VMEM(shape, F32)
    heads = (HEADS_DEV, ROWS, HEAD)
    piece = (PIECE_ROWS, PIECE_COLS)
    return pl.pallas_call(
        sublayer_kernel,
        out_shape=tuple([jax.ShapeDtypeStruct(block, BF16)] * 4)
        + (jax.ShapeDtypeStruct((COLS, FEATURES), BF16),),
        in_specs=[VMEM] * 6,
        out_specs=(VMEM,) * 5,
        scratch_shapes=[
            pltpu.VMEM((WINDOW, 1, ROWS), jnp.int32),
            pltpu.VMEM((ROWS, 128), jnp.int32),
            bf16(WINDOW, 2, *block),
            bf16(TP, *block),
            bf16(*block),
            f32(*block),
            f32(*heads),
            f32(*heads),
            f32(*heads),
            f32(ROWS, HEAD),
            f32(ROWS, HEAD),
            f32(ROWS, HEAD),
            bf16(*block),
            bf16(COLS, ROWS),
            bf16(WINDOW, 2, *block),
            f32(2, *block),
            bf16(4, 2, *block),
            bf16(TP, *block),
            bf16(2, 2, HALF, COLS),
            bf16(2, 2, *block),
            bf16(2, 2, HALF, COLS),
            bf16(2, *block),
            bf16(HEADS_DEV, 2, 4, 4, *piece),
            bf16(HEADS_DEV, 4, 4, *piece),
            bf16(HEADS_DEV, 4, 4, *piece),
            bf16(HEADS_DEV, 2, 2, *piece),
            bf16(HEADS_DEV, 2, 4, *piece),
            bf16(HEADS_DEV, 4, *piece),
            bf16(HEADS_DEV, 3, *piece),
            pltpu.SemaphoreType.DMA((ROLES,)),
            pltpu.SemaphoreType.DMA((ROLES,)),
        ],
        compiler_params=pltpu.CompilerParams(
            collective_id=0, has_side_effects=True, vmem_limit_bytes=LIMIT
        ),
        name="sublayer",
    )(ids, query, keys, values, cotangent, weight)


def hand_over_kernel(*refs):
    count = len(refs) // 2
    for n in range(count):
        refs[count + n][...] = refs[n][...]


def hand_over(arrays):
    return pl.pallas_call(
        hand_over_kernel,
        out_shape=tuple(jax.ShapeDtypeStruct(a.shape, a.dtype) for a in arrays),
        in_specs=[VMEM] * len(arrays),
        out_specs=(VMEM,) * len(arrays),
        name="hand_over",
    )(*arrays)


def on_device(query, keys, values, image_ids, out_weight, cotangent):
    return hand_over(sublayer(image_ids, query, keys, values, cotangent, out_weight))


def solution(mesh):
    placed = (
        P("ctx", "tp"),
        P("ctx", "tp"),
        P("ctx", "tp"),
        P("ctx"),
        P("tp", None),
        P("ctx", "tp"),
    )
    return jax.shard_map(
        on_device,
        mesh=mesh,
        in_specs=placed,
        out_specs=(P("ctx", "tp"), P("ctx", "tp"), P("ctx", "tp"), P("ctx", "tp"), P("tp", None)),
        check_vma=False,
    )
```

```python
import functools

import jax
import jax.numpy as jnp
from jax import lax
from jax.experimental import pallas as pl
from jax.experimental.pallas import tpu as pltpu
from jax.sharding import PartitionSpec as P

HEAD = 128
ROWS = 512
COLS = 384
HEADS_DEV = COLS // HEAD
TP = 8
FEATURES = TP * COLS
WINDOW = 5
OWN = 2
CHUNK = 256
HALF = ROWS // 2
PIECE_ROWS = 16
PIECE_COLS = 768
NEG = -1e30
SCALE = HEAD ** -0.5
EXP2_SCALE = SCALE * 1.4426950408889634
F32 = jnp.float32
BF16 = jnp.bfloat16
MESH = pl.DeviceIdType.MESH
VMEM = pl.BlockSpec(memory_space=pltpu.VMEM)
ANY = pl.BlockSpec(memory_space=pl.ANY)
LIMIT = 60 * 1024 * 1024


class Links:
    def __init__(self, send_sem, recv_sem):
        self.send_sem, self.recv_sem = send_sem, recv_sem
        self.sent = []

    def _copy(self, src, dst, role, where):
        return pltpu.make_async_remote_copy(
            src_ref=src,
            dst_ref=dst,
            send_sem=self.send_sem.at[role],
            recv_sem=self.recv_sem.at[role],
            device_id=where,
            device_id_type=MESH,
        )

    def send(self, src, dst, role, where, keep=True):
        copy = self._copy(src, dst, role, where)
        copy.start()
        if keep:
            self.sent.append(copy)

    def arrive(self, dst, role, where):
        self._copy(dst, dst, role, where).wait_recv()

    def left(self, src, role, where):
        self._copy(src, src, role, where).wait_send()

    def finish(self):
        for copy in self.sent:
            copy.wait_send()


def greet(peers):
    barrier = pltpu.get_barrier_semaphore()
    for where in peers:
        pl.semaphore_signal(barrier, inc=1, device_id=where, device_id_type=MESH)
    pl.semaphore_wait(barrier, len(peers))


def ctx_ring(place, step):
    return {"ctx": lax.rem(place + step + 32, 32)}


def columns(index):
    return pl.ds(pl.multiple_of(index * COLS, COLS), COLS)


IDS, KV, COT, DKV, MIX, FAR, SUM, ROLES = 0, 4, 16, 28, 40, 52, 53, 116
CORE, XR, ZR, ZG, XG, CG, SUM_ROLES = 0, 1, 7, 10, 13, 17, 21


def dot(a, b, contract):
    return lax.dot_general(
        a, b, ((contract[:1], contract[1:]), ((), ())), preferred_element_type=F32
    )


def wide(x, times):
    return jnp.concatenate([x] * times, axis=1)


def head_columns(h):
    return pl.ds(pl.multiple_of(h * HEAD, HEAD), HEAD)


def sublayer_kernel(
    ids_ref, q_ref, k_ref, v_ref, cot_ref, w_ref,
    mixed_ref, gq_ref, gk_ref, gv_ref, gw_ref,
    ids_all, ids_col, kv_all, cot_all, d_att, d_acc,
    top_ref, total_ref, out_acc, lse_ref, delta_ref, dq_acc, att, att_t,
    dkv, own, dkv_in,
    m_ref, m_hop, m_in, m_out, m_far,
    w_part, w_core, w_sum, w_hop, w_in, w_x, w_z,
    send_sem, recv_sem,
):
    place = lax.axis_index("ctx")
    part = lax.axis_index("tp")
    core = lax.rem(place, 2)
    z = lax.rem(lax.div(place, 2), 4)
    x = lax.div(place, 8)
    high = lax.rem(part, 2)
    flip = 1 - 2 * high
    after, before = ctx_ring(place, 2), ctx_ring(place, -2)
    sibling = {"ctx": place + 1 - 2 * core}
    x_up, x_down = ctx_ring(place, 8), ctx_ring(place, -8)
    z_to = [{"ctx": 8 * x + 2 * lax.rem(z + d, 4) + core} for d in (1, 2, 3)]
    z_from = [{"ctx": 8 * x + 2 * lax.rem(z + 4 - d, 4) + core} for d in (1, 2, 3)]
    up, down = lax.rem(part + 2, TP), lax.rem(part + 6, TP)
    across = lax.rem(part + 4, TP)
    over = part + flip
    y_up, y_down, far = {"tp": up}, {"tp": down}, {"tp": over}
    low, top = pl.ds(0, HALF), pl.ds(HALF, HALF)
    z_low, z_top = pl.ds(0, 2), pl.ds(2, 2)
    sib_slot, relay_slot = 3 - 2 * core, 1 + 2 * core
    direct_slot, sum_slot = 4 * core, 4 - 4 * core
    direct_to = {"ctx": lax.rem(place + 30 + 4 * core, 32)}
    sum_to = {"ctx": lax.rem(place + 34 - 4 * core, 32)}

    kv_all[OWN, 0] = k_ref[...]
    kv_all[OWN, 1] = v_ref[...]
    ids_all[OWN] = ids_ref[...].reshape(1, ROWS)
    greet([after, before, sibling, x_up, x_down, y_up, y_down, far] + z_to)
    links = Links(send_sem, recv_sem)

    links.send(cot_ref.at[low], cot_all.at[part, low], COT, far)
    links.send(cot_ref.at[top], cot_all.at[part, top], COT + 9, far)
    links.send(cot_ref, cot_all.at[part], COT + 1, y_up)
    links.send(cot_ref, cot_all.at[part], COT + 2, y_down)
    links.send(ids_all.at[OWN], ids_all.at[0], IDS, after)
    links.send(ids_all.at[OWN], ids_all.at[4], IDS + 1, before)
    links.send(ids_all.at[OWN], ids_all.at[relay_slot], IDS + 2, sibling)

    def send_heads(h):
        mine = kv_all.at[OWN, :, :, head_columns(h)]
        role = KV + 4 * h
        links.send(mine, kv_all.at[0, :, :, head_columns(h)], role, after, False)
        links.send(mine, kv_all.at[4, :, :, head_columns(h)], role + 1, before, False)
        links.send(mine, kv_all.at[relay_slot, :, :, head_columns(h)], role + 2, sibling, False)

    send_heads(0)
    for n in range(ROWS // 128):
        piece = jnp.broadcast_to(ids_all[OWN, :, pl.ds(n * 128, 128)], (128, 128))
        ids_col[pl.ds(n * 128, 128), :] = jnp.transpose(piece)
    cot_all[part] = cot_ref[...]

    def project(block, first=False):
        term = dot(cot_all[block], w_ref[:, columns(block)], (1, 1))
        if first:
            d_acc[...] = term
        else:
            d_acc[...] += term

    def key_ids(slot):
        return ids_all[slot]

    def scores(h, slot):
        cols = head_columns(h)
        s = dot(q_ref[:, cols], kv_all[slot, 0, :, cols], (1, 1)) * EXP2_SCALE
        return jnp.where(wide(ids_col[...], ROWS // 128) == key_ids(slot), s, NEG)

    def lanes(op, s):
        return functools.reduce(op, [s[:, n : n + 128] for n in range(0, ROWS, 128)])

    def attend(h, slot, first=False):
        s = scores(h, slot)
        peak = jnp.max(lanes(jnp.maximum, s), axis=1, keepdims=True)
        peak = jnp.broadcast_to(peak, (ROWS, 128))
        if not first:
            old = top_ref[h]
            peak = jnp.maximum(old, peak)
            fade = jnp.exp2(old - peak)
        p = jnp.exp2(s - wide(peak, ROWS // 128))
        part_total = lanes(jnp.add, p)
        term = dot(p.astype(BF16), kv_all[slot, 1, :, head_columns(h)], (1, 0))
        if not first:
            part_total += total_ref[h] * fade
            term += out_acc[h] * fade
        total_ref[h] = part_total
        out_acc[h] = term
        top_ref[h] = peak

    def settle(h):
        cols = head_columns(h)
        total = jnp.sum(total_ref[h], axis=1, keepdims=True)
        attended = out_acc[h] * (1.0 / total)
        att_t[cols, :] = jnp.transpose(attended).astype(BF16)
        attended = attended.astype(BF16)
        att[:, cols] = attended
        lse_ref[...] = top_ref[h] + jnp.broadcast_to(jnp.log2(total), (ROWS, 128))
        delta = jnp.sum(
            attended.astype(F32) * d_att[:, cols].astype(F32), axis=1, keepdims=True
        )
        delta_ref[...] = jnp.broadcast_to(delta, (ROWS, 128))

    def back(h, slot, first=False, last=False):
        cols = head_columns(h)
        q, g = q_ref[:, cols], d_att[:, cols]
        k, v = kv_all[slot, 0, :, cols], kv_all[slot, 1, :, cols]
        weight = jnp.exp2(scores(h, slot) - wide(lse_ref[...], ROWS // 128))
        dots = dot(g, v, (1, 1))
        dscores = (weight * (dots - wide(delta_ref[...], ROWS // 128))).astype(BF16)
        dk = dot(dscores, q, (0, 0)) * SCALE
        dv = dot(weight.astype(BF16), g, (0, 0))
        dq = dot(dscores, k, (1, 0))
        if not first:
            dq += dq_acc[...]
        if last:
            own[0, :, cols] = dk
            own[1, :, cols] = dv
            gq_ref[:, cols] = (dq * SCALE).astype(BF16)
        else:
            dkv[slot, 0, :, cols] = dk.astype(BF16)
            dkv[slot, 1, :, cols] = dv.astype(BF16)
            dq_acc[...] = dq

    def each_head(work):
        def step(h, carry):
            work(h)
            return carry

        lax.fori_loop(0, HEADS_DEV, step, 0)

    def send_half(block, half, role, where):
        links.send(cot_all.at[block, half], cot_all.at[block, half], role, where, False)

    def halves(block, role):
        links.arrive(cot_all.at[block, low], role, y_down)
        links.arrive(cot_all.at[block, top], role + 1, y_up)

    project(part, first=True)
    each_head(lambda h: attend(h, OWN, first=True))
    links.arrive(cot_all.at[down], COT + 1, y_down)
    send_half(down, low, COT + 3, y_up)
    links.arrive(cot_all.at[up], COT + 2, y_up)
    send_half(up, top, COT + 4, y_down)
    send_heads(1)
    project(down)
    project(up)
    links.arrive(ids_all.at[0], IDS, before)
    links.arrive(ids_all.at[4], IDS + 1, after)
    links.send(ids_all.at[sum_slot], ids_all.at[sib_slot], IDS + 3, sibling)
    links.arrive(cot_all.at[over, low], COT, far)
    send_half(over, low, COT + 5, y_up)
    send_half(over, low, COT + 6, y_down)
    links.arrive(cot_all.at[over, top], COT + 9, far)
    send_half(over, top, COT + 10, y_up)
    send_half(over, top, COT + 11, y_down)
    project(over)
    send_heads(2)
    links.arrive(ids_all.at[sib_slot], IDS + 2, sibling)

    def attend_sibling(h):
        links.arrive(kv_all.at[sib_slot, :, :, head_columns(h)], KV + 4 * h + 2, sibling)
        attend(h, sib_slot)

    each_head(attend_sibling)
    halves(across, COT + 3)
    project(across)
    links.arrive(ids_all.at[relay_slot], IDS + 3, sibling)

    down_over, up_over, across_over = down + flip, up + flip, across + flip
    links.arrive(cot_all.at[down_over, low], COT + 5, y_down)
    send_half(down_over, low, COT + 7, y_up)
    links.arrive(cot_all.at[up_over, top], COT + 11, y_up)
    send_half(up_over, top, COT + 8, y_down)

    def rest_of_cotangent():
        links.arrive(cot_all.at[down_over, top], COT + 10, y_down)
        links.arrive(cot_all.at[up_over, low], COT + 6, y_up)
        project(down_over)
        project(up_over)
        halves(across_over, COT + 7)
        project(across_over)
        d_att[...] = d_acc[...].astype(BF16)

    planes = (0, flip)

    def share_plane(n):
        add = planes[n]
        role = MIX + 6 * n

        def mix(block):
            m_ref[block] = dot(att[...], w_ref[:, columns(block)], (1, 0)).astype(BF16)

        mix(across + add)
        links.send(m_ref.at[across + add, low], m_hop.at[n, 0], role, y_up, False)
        links.send(m_ref.at[across + add, top], m_hop.at[n, 1], role + 1, y_down, False)
        mix(up + add)
        links.send(m_ref.at[up + add, top], m_in.at[n, 0, top], role + 2, y_up, False)
        mix(down + add)
        links.send(m_ref.at[down + add, low], m_in.at[n, 1, low], role + 3, y_down, False)
        mix(part + add)

    def plane_hops(n):
        add = planes[n]
        role = MIX + 6 * n
        links.arrive(m_hop.at[n, 0], role, y_down)
        m_out[n, 0] = add_up(m_ref[up + add, low], m_hop[n, 0])
        links.send(m_out.at[n, 0], m_in.at[n, 0, low], role + 4, y_up, False)
        links.arrive(m_hop.at[n, 1], role + 1, y_up)
        m_out[n, 1] = add_up(m_ref[down + add, top], m_hop[n, 1])
        links.send(m_out.at[n, 1], m_in.at[n, 1, top], role + 5, y_down, False)

    def quarter(step):
        return lax.rem(x + step, 4)

    below, above, opposite = quarter(3), quarter(1), quarter(2)

    def weight_rows(h):
        rows = head_columns(h)

        def two_blocks(n, carry):
            for side in range(2):
                term = dot(att_t[rows, :], cot_all[2 * n + side], (1, 0)).astype(BF16)
                side_cols = pl.ds(side * COLS, COLS)
                for c in range(2):
                    for j in range(4):
                        first = (4 * c + j) * PIECE_ROWS
                        w_part[h, c, n, j, :, side_cols] = term[first : first + PIECE_ROWS]
            return carry

        lax.fori_loop(0, 4, two_blocks, 0)
        links.send(
            w_part.at[h, 1 - core], w_core.at[h], SUM + SUM_ROLES * h + CORE, sibling, False
        )

    def out_rows(h, c, first, count):
        start = h * HEAD + c * (HEAD // 2) + first * PIECE_ROWS
        return pl.ds(pl.multiple_of(start, PIECE_ROWS), count * PIECE_ROWS)

    def out_cols(block):
        return pl.ds(pl.multiple_of(block * PIECE_COLS, PIECE_COLS), PIECE_COLS)

    def add_up(*terms):
        return sum(t.astype(F32) for t in terms).astype(BF16)

    def sum_cores(h):
        role = SUM + SUM_ROLES * h
        links.arrive(w_core.at[h], role + CORE, sibling)

        def add(i, carry):
            w_sum[h, i] = add_up(w_part[h, core, i], w_core[h, i])
            return carry

        lax.fori_loop(0, 4, add, 0)
        role += XR
        links.send(w_sum.at[h, opposite, z_low], w_hop.at[h, 0], role, x_up, False)
        links.send(w_sum.at[h, opposite, z_top], w_hop.at[h, 1], role + 1, x_down, False)
        links.send(w_sum.at[h, above, z_top], w_in.at[h, 0, z_top], role + 2, x_up, False)
        links.send(w_sum.at[h, below, z_low], w_in.at[h, 1, z_low], role + 3, x_down, False)

    def sum_hops(h):
        role = SUM + SUM_ROLES * h + XR
        links.arrive(w_hop.at[h, 0], role, x_down)
        w_hop[h, 0] = add_up(w_sum[h, above, z_low], w_hop[h, 0])
        links.send(w_hop.at[h, 0], w_in.at[h, 0, z_low], role + 4, x_up, False)
        links.arrive(w_hop.at[h, 1], role + 1, x_up)
        w_hop[h, 1] = add_up(w_sum[h, below, z_top], w_hop[h, 1])
        links.send(w_hop.at[h, 1], w_in.at[h, 1, z_top], role + 5, x_down, False)

    def sum_x(h):
        role = SUM + SUM_ROLES * h + XR
        links.arrive(w_in.at[h, 0, z_top], role + 2, x_down)
        links.arrive(w_in.at[h, 1, z_low], role + 3, x_up)
        links.arrive(w_in.at[h, 0, z_low], role + 4, x_down)
        links.arrive(w_in.at[h, 1, z_top], role + 5, x_up)
        w_x[h] = add_up(w_sum[h, x], w_in[h, 0], w_in[h, 1])
        role = SUM + SUM_ROLES * h + ZR
        for d in range(3):
            links.send(w_x.at[h, lax.rem(z + d + 1, 4)], w_z.at[h, d], role + d, z_to[d], False)

    def sum_z(h):
        role = SUM + SUM_ROLES * h + ZR
        for d in range(3):
            links.arrive(w_z.at[h, d], role + d, z_from[d])
        mine = gw_ref.at[out_rows(h, core, z, 1), out_cols(x)]
        mine[...] = add_up(w_x[h, z], w_z[h, 0], w_z[h, 1], w_z[h, 2])
        role = SUM + SUM_ROLES * h + ZG
        for d in range(3):
            links.send(mine, mine, role + d, z_to[d], False)

    def spread_x(h):
        role = SUM + SUM_ROLES * h
        for d in range(3):
            rows = out_rows(h, core, lax.rem(z + 3 - d, 4), 1)
            links.arrive(gw_ref.at[rows, out_cols(x)], role + ZG + d, z_from[d])
        mine = gw_ref.at[out_rows(h, core, 0, 4), out_cols(x)]
        links.send(mine, mine, role + XG, x_up, False)
        links.send(mine, mine, role + XG + 1, x_down, False)
        links.send(mine, mine, role + CG, sibling, False)

    def spread_on(h):
        role = SUM + SUM_ROLES * h
        for n, (block, back_from, on_to) in enumerate(((below, x_down, x_up), (above, x_up, x_down))):
            whole = gw_ref.at[out_rows(h, core, 0, 4), out_cols(block)]
            part_of = gw_ref.at[out_rows(h, core, 2 * n, 2), out_cols(block)]
            links.arrive(whole, role + XG + n, back_from)
            links.send(part_of, part_of, role + XG + 2 + n, on_to, False)
            links.send(whole, whole, role + CG + 1 + n, sibling, False)

    def spread_cores(h):
        role = SUM + SUM_ROLES * h
        for n, back_from in enumerate((x_down, x_up)):
            part_of = gw_ref.at[out_rows(h, core, 2 * n, 2), out_cols(opposite)]
            links.arrive(part_of, role + XG + 2 + n, back_from)
        whole = gw_ref.at[out_rows(h, core, 0, 4), out_cols(opposite)]
        links.send(whole, whole, role + CG + 3, sibling, False)

    def spread_done(h):
        role = SUM + SUM_ROLES * h + CG
        for n, block in enumerate((x, below, above, opposite)):
            links.arrive(gw_ref.at[out_rows(h, 1 - core, 0, 4), out_cols(block)], role + n, sibling)

    def sum_left(h):
        role = SUM + SUM_ROLES * h
        links.left(w_core.at[h], role + CORE, sibling)
        for n in range(6):
            links.left(w_hop.at[h, 0], role + XR + n, x_up)
        for n in range(3):
            links.left(w_z.at[h, n], role + ZR + n, z_to[n])
            links.left(w_z.at[h, n], role + ZG + n, z_to[n])
        whole = gw_ref.at[out_rows(h, core, 0, 4), out_cols(x)]
        half = gw_ref.at[out_rows(h, core, 0, 2), out_cols(x)]
        for n in range(2):
            links.left(whole, role + XG + n, x_up)
            links.left(half, role + XG + 2 + n, x_up)
        for n in range(4):
            links.left(whole, role + CG + n, sibling)

    final = HEADS_DEV - 1

    def per_head(h):
        def of_last(step):
            pl.when(h > 0)(lambda: step(h - 1))

        cols = head_columns(h)
        role = KV + 4 * h
        links.arrive(kv_all.at[0, :, :, cols], role, before)
        links.arrive(kv_all.at[4, :, :, cols], role + 1, after)
        links.send(
            kv_all.at[sum_slot, :, :, cols], kv_all.at[sib_slot, :, :, cols], role + 3, sibling,
            False,
        )
        attend(h, 0)
        attend(h, 4)
        pl.when(h == 0)(rest_of_cotangent)
        links.arrive(kv_all.at[relay_slot, :, :, cols], role + 3, sibling)
        attend(h, relay_slot)
        settle(h)
        weight_rows(h)
        pl.when(h == final)(lambda: share_plane(1))
        role = DKV + 4 * h
        back(h, relay_slot, first=True)
        links.send(
            dkv.at[relay_slot, :, :, cols], dkv_in.at[1, :, :, cols], role + 1, sibling, False
        )
        sum_cores(h)
        back(h, direct_slot)
        links.send(
            dkv.at[direct_slot, :, :, cols], dkv_in.at[2 + core, :, :, cols], role + 2 + core,
            direct_to, False,
        )
        back(h, sum_slot)
        links.arrive(dkv_in.at[1, :, :, cols], role + 1, sibling)
        for n in range(2):
            dkv[sum_slot, n, :, cols] = add_up(
                dkv[sum_slot, n, :, cols], dkv_in[1, n, :, cols]
            )
        links.send(
            dkv.at[sum_slot, :, :, cols], dkv_in.at[3 - core, :, :, cols], role + 3 - core,
            sum_to, False,
        )
        sum_hops(h)
        back(h, sib_slot)
        links.send(dkv.at[sib_slot, :, :, cols], dkv_in.at[0, :, :, cols], role, sibling, False)
        pl.when(h == final)(lambda: plane_hops(1))
        back(h, OWN, last=True)
        sum_x(h)
        of_last(sum_z)

    each_head(per_head)

    def along_y(n):
        add = planes[n]
        role = MIX + 6 * n
        links.arrive(m_in.at[n, 0, top], role + 2, y_down)
        links.arrive(m_in.at[n, 1, low], role + 3, y_up)
        links.arrive(m_in.at[n, 0, low], role + 4, y_down)
        links.arrive(m_in.at[n, 1, top], role + 5, y_up)
        return add_up(m_ref[part + add], m_in[n, 0], m_in[n, 1])

    def add_keys(h):
        cols = head_columns(h)
        role = DKV + 4 * h
        links.arrive(dkv_in.at[0, :, :, cols], role, sibling)
        links.arrive(dkv_in.at[2, :, :, cols], role + 2, after)
        links.arrive(dkv_in.at[3, :, :, cols], role + 3, before)
        for n, out in enumerate((gk_ref, gv_ref)):
            out[:, cols] = add_up(
                own[n, :, cols], dkv_in[0, n, :, cols], dkv_in[2, n, :, cols],
                dkv_in[3, n, :, cols],
            )

    share_plane(0)
    sum_z(final)
    spread_x(0)
    spread_x(1)
    plane_hops(0)
    spread_on(0)
    spread_on(1)
    spread_x(final)
    m_far[0] = along_y(1)
    links.send(m_far.at[0], m_far.at[1], FAR, far)
    spread_cores(0)
    spread_cores(1)
    m_in[0, 0] = along_y(0)
    spread_on(final)
    each_head(add_keys)
    spread_cores(final)
    links.arrive(m_far.at[1], FAR, far)
    mixed_ref[...] = add_up(m_in[0, 0], m_far[1])
    each_head(spread_done)

    def heads_left(h):
        cols = head_columns(h)
        for n in range(4):
            links.left(kv_all.at[OWN, :, :, cols], KV + 4 * h + n, sibling)
            links.left(dkv.at[OWN, :, :, cols], DKV + 4 * h + n, sibling)
        sum_left(h)

    each_head(heads_left)
    for n in range(2):
        for k in range(6):
            links.left(m_hop.at[n, 0], MIX + 6 * n + k, y_up)
    for role in (3, 4, 5, 6, 7, 8, 10, 11):
        links.left(cot_all.at[0, low], COT + role, y_up)
    links.finish()


def sublayer(ids, query, keys, values, cotangent, weight):
    block = (ROWS, COLS)
    bf16 = lambda *shape: pltpu.VMEM(shape, BF16)
    f32 = lambda *shape: pltpu.VMEM(shape, F32)
    heads = (HEADS_DEV, ROWS, HEAD)
    piece = (PIECE_ROWS, PIECE_COLS)
    return pl.pallas_call(
        sublayer_kernel,
        out_shape=tuple([jax.ShapeDtypeStruct(block, BF16)] * 4)
        + (jax.ShapeDtypeStruct((COLS, FEATURES), BF16),),
        in_specs=[VMEM] * 6,
        out_specs=(VMEM,) * 5,
        scratch_shapes=[
            pltpu.VMEM((WINDOW, 1, ROWS), jnp.int32),
            pltpu.VMEM((ROWS, 128), jnp.int32),
            bf16(WINDOW, 2, *block),
            bf16(TP, *block),
            bf16(*block),
            f32(*block),
            f32(*heads),
            f32(*heads),
            f32(*heads),
            f32(ROWS, HEAD),
            f32(ROWS, HEAD),
            f32(ROWS, HEAD),
            bf16(*block),
            bf16(COLS, ROWS),
            bf16(WINDOW, 2, *block),
            f32(2, *block),
            bf16(4, 2, *block),
            bf16(TP, *block),
            bf16(2, 2, HALF, COLS),
            bf16(2, 2, *block),
            bf16(2, 2, HALF, COLS),
            bf16(2, *block),
            bf16(HEADS_DEV, 2, 4, 4, *piece),
            bf16(HEADS_DEV, 4, 4, *piece),
            bf16(HEADS_DEV, 4, 4, *piece),
            bf16(HEADS_DEV, 2, 2, *piece),
            bf16(HEADS_DEV, 2, 4, *piece),
            bf16(HEADS_DEV, 4, *piece),
            bf16(HEADS_DEV, 3, *piece),
            pltpu.SemaphoreType.DMA((ROLES,)),
            pltpu.SemaphoreType.DMA((ROLES,)),
        ],
        compiler_params=pltpu.CompilerParams(
            collective_id=0, has_side_effects=True, vmem_limit_bytes=LIMIT
        ),
        name="sublayer",
    )(ids, query, keys, values, cotangent, weight)


def hand_over_kernel(*refs):
    count = len(refs) // 2
    for n in range(count):
        refs[count + n][...] = refs[n][...]


def hand_over(arrays):
    return pl.pallas_call(
        hand_over_kernel,
        out_shape=tuple(jax.ShapeDtypeStruct(a.shape, a.dtype) for a in arrays),
        in_specs=[VMEM] * len(arrays),
        out_specs=(VMEM,) * len(arrays),
        name="hand_over",
    )(*arrays)


def on_device(query, keys, values, image_ids, out_weight, cotangent):
    return hand_over(sublayer(image_ids, query, keys, values, cotangent, out_weight))


def solution(mesh):
    placed = (
        P("ctx", "tp"),
        P("ctx", "tp"),
        P("ctx", "tp"),
        P("ctx"),
        P("tp", None),
        P("ctx", "tp"),
    )
    return jax.shard_map(
        on_device,
        mesh=mesh,
        in_specs=placed,
        out_specs=(P("ctx", "tp"), P("ctx", "tp"), P("ctx", "tp"), P("ctx", "tp"), P("tp", None)),
        check_vma=False,
    )
```

```python
import functools

import jax
import jax.numpy as jnp
from jax import lax
from jax.experimental import pallas as pl
from jax.experimental.pallas import tpu as pltpu
from jax.sharding import PartitionSpec as P

HEAD = 128
ROWS = 512
COLS = 384
HEADS_DEV = COLS // HEAD
TP = 8
FEATURES = TP * COLS
WINDOW = 5
OWN = 2
CHUNK = 256
HALF = ROWS // 2
PIECE_ROWS = 16
PIECE_COLS = 768
NEG = -1e30
SCALE = HEAD ** -0.5
EXP2_SCALE = SCALE * 1.4426950408889634
F32 = jnp.float32
BF16 = jnp.bfloat16
MESH = pl.DeviceIdType.MESH
VMEM = pl.BlockSpec(memory_space=pltpu.VMEM)
ANY = pl.BlockSpec(memory_space=pl.ANY)
LIMIT = 60 * 1024 * 1024


class Links:
    def __init__(self, send_sem, recv_sem):
        self.send_sem, self.recv_sem = send_sem, recv_sem
        self.sent = []

    def _copy(self, src, dst, role, where):
        return pltpu.make_async_remote_copy(
            src_ref=src,
            dst_ref=dst,
            send_sem=self.send_sem.at[role],
            recv_sem=self.recv_sem.at[role],
            device_id=where,
            device_id_type=MESH,
        )

    def send(self, src, dst, role, where, keep=True):
        copy = self._copy(src, dst, role, where)
        copy.start()
        if keep:
            self.sent.append(copy)

    def arrive(self, dst, role, where):
        self._copy(dst, dst, role, where).wait_recv()

    def left(self, src, role, where):
        self._copy(src, src, role, where).wait_send()

    def finish(self):
        for copy in self.sent:
            copy.wait_send()


def greet(peers):
    barrier = pltpu.get_barrier_semaphore()
    for where in peers:
        pl.semaphore_signal(barrier, inc=1, device_id=where, device_id_type=MESH)
    pl.semaphore_wait(barrier, len(peers))


def ctx_ring(place, step):
    return {"ctx": lax.rem(place + step + 32, 32)}


def columns(index):
    return pl.ds(pl.multiple_of(index * COLS, COLS), COLS)


IDS, KV, COT, DKV, MIX, FAR, SUM, ROLES = 0, 4, 16, 28, 40, 52, 53, 116
CORE, XR, ZR, ZG, XG, CG, SUM_ROLES = 0, 1, 7, 10, 13, 17, 21


def dot(a, b, contract):
    return lax.dot_general(
        a, b, ((contract[:1], contract[1:]), ((), ())), preferred_element_type=F32
    )


def wide(x, times):
    return jnp.concatenate([x] * times, axis=1)


def head_columns(h):
    return pl.ds(pl.multiple_of(h * HEAD, HEAD), HEAD)


def sublayer_kernel(
    ids_ref, q_ref, k_ref, v_ref, cot_ref, w_ref,
    mixed_ref, gq_ref, gk_ref, gv_ref, gw_ref,
    ids_all, ids_col, kv_all, cot_all, d_att, d_acc,
    top_ref, total_ref, out_acc, lse_ref, delta_ref, dq_acc, att, att_t,
    dkv, own, dkv_in,
    m_ref, m_hop, m_in, m_out, m_far,
    w_part, w_core, w_sum, w_hop, w_in, w_x, w_z,
    send_sem, recv_sem,
):
    place = lax.axis_index("ctx")
    part = lax.axis_index("tp")
    core = lax.rem(place, 2)
    z = lax.rem(lax.div(place, 2), 4)
    x = lax.div(place, 8)
    high = lax.rem(part, 2)
    flip = 1 - 2 * high
    after, before = ctx_ring(place, 2), ctx_ring(place, -2)
    sibling = {"ctx": place + 1 - 2 * core}
    x_up, x_down = ctx_ring(place, 8), ctx_ring(place, -8)
    z_to = [{"ctx": 8 * x + 2 * lax.rem(z + d, 4) + core} for d in (1, 2, 3)]
    z_from = [{"ctx": 8 * x + 2 * lax.rem(z + 4 - d, 4) + core} for d in (1, 2, 3)]
    up, down = lax.rem(part + 2, TP), lax.rem(part + 6, TP)
    across = lax.rem(part + 4, TP)
    over = part + flip
    y_up, y_down, far = {"tp": up}, {"tp": down}, {"tp": over}
    low, top = pl.ds(0, HALF), pl.ds(HALF, HALF)
    z_low, z_top = pl.ds(0, 2), pl.ds(2, 2)
    sib_slot, relay_slot = 3 - 2 * core, 1 + 2 * core
    direct_slot, sum_slot = 4 * core, 4 - 4 * core
    direct_to = {"ctx": lax.rem(place + 30 + 4 * core, 32)}
    sum_to = {"ctx": lax.rem(place + 34 - 4 * core, 32)}

    kv_all[OWN, 0] = k_ref[...]
    kv_all[OWN, 1] = v_ref[...]
    ids_all[OWN] = ids_ref[...].reshape(1, ROWS)
    greet([after, before, sibling, x_up, x_down, y_up, y_down, far] + z_to)
    links = Links(send_sem, recv_sem)

    links.send(cot_ref.at[low], cot_all.at[part, low], COT, far)
    links.send(cot_ref.at[top], cot_all.at[part, top], COT + 9, far)
    links.send(cot_ref, cot_all.at[part], COT + 1, y_up)
    links.send(cot_ref, cot_all.at[part], COT + 2, y_down)
    links.send(ids_all.at[OWN], ids_all.at[0], IDS, after)
    links.send(ids_all.at[OWN], ids_all.at[4], IDS + 1, before)
    links.send(ids_all.at[OWN], ids_all.at[relay_slot], IDS + 2, sibling)

    def send_heads(h):
        mine = kv_all.at[OWN, :, :, head_columns(h)]
        role = KV + 4 * h
        links.send(mine, kv_all.at[0, :, :, head_columns(h)], role, after, False)
        links.send(mine, kv_all.at[4, :, :, head_columns(h)], role + 1, before, False)
        links.send(mine, kv_all.at[relay_slot, :, :, head_columns(h)], role + 2, sibling, False)

    send_heads(0)
    for n in range(ROWS // 128):
        piece = jnp.broadcast_to(ids_all[OWN, :, pl.ds(n * 128, 128)], (128, 128))
        ids_col[pl.ds(n * 128, 128), :] = jnp.transpose(piece)
    cot_all[part] = cot_ref[...]

    def project(block, first=False):
        term = dot(cot_all[block], w_ref[:, columns(block)], (1, 1))
        if first:
            d_acc[...] = term
        else:
            d_acc[...] += term

    def key_ids(slot):
        return ids_all[slot]

    def scores(h, slot):
        cols = head_columns(h)
        s = dot(q_ref[:, cols], kv_all[slot, 0, :, cols], (1, 1)) * EXP2_SCALE
        return jnp.where(wide(ids_col[...], ROWS // 128) == key_ids(slot), s, NEG)

    def lanes(op, s):
        return functools.reduce(op, [s[:, n : n + 128] for n in range(0, ROWS, 128)])

    def attend(h, slot, first=False):
        s = scores(h, slot)
        peak = jnp.max(lanes(jnp.maximum, s), axis=1, keepdims=True)
        peak = jnp.broadcast_to(peak, (ROWS, 128))
        if not first:
            old = top_ref[h]
            peak = jnp.maximum(old, peak)
            fade = jnp.exp2(old - peak)
        p = jnp.exp2(s - wide(peak, ROWS // 128))
        part_total = lanes(jnp.add, p)
        term = dot(p.astype(BF16), kv_all[slot, 1, :, head_columns(h)], (1, 0))
        if not first:
            part_total += total_ref[h] * fade
            term += out_acc[h] * fade
        total_ref[h] = part_total
        out_acc[h] = term
        top_ref[h] = peak

    def settle(h):
        cols = head_columns(h)
        total = jnp.sum(total_ref[h], axis=1, keepdims=True)
        attended = out_acc[h] * (1.0 / total)
        att_t[cols, :] = jnp.transpose(attended).astype(BF16)
        attended = attended.astype(BF16)
        att[:, cols] = attended
        lse_ref[...] = top_ref[h] + jnp.broadcast_to(jnp.log2(total), (ROWS, 128))
        delta = jnp.sum(
            attended.astype(F32) * d_att[:, cols].astype(F32), axis=1, keepdims=True
        )
        delta_ref[...] = jnp.broadcast_to(delta, (ROWS, 128))

    def back(h, slot, first=False, last=False):
        cols = head_columns(h)
        q, g = q_ref[:, cols], d_att[:, cols]
        k, v = kv_all[slot, 0, :, cols], kv_all[slot, 1, :, cols]
        weight = jnp.exp2(scores(h, slot) - wide(lse_ref[...], ROWS // 128))
        dots = dot(g, v, (1, 1))
        dscores = (weight * (dots - wide(delta_ref[...], ROWS // 128))).astype(BF16)
        dk = dot(dscores, q, (0, 0)) * SCALE
        dv = dot(weight.astype(BF16), g, (0, 0))
        dq = dot(dscores, k, (1, 0))
        if not first:
            dq += dq_acc[...]
        if last:
            own[0, :, cols] = dk
            own[1, :, cols] = dv
            gq_ref[:, cols] = (dq * SCALE).astype(BF16)
        else:
            dkv[slot, 0, :, cols] = dk.astype(BF16)
            dkv[slot, 1, :, cols] = dv.astype(BF16)
            dq_acc[...] = dq

    def each_head(work):
        def step(h, carry):
            work(h)
            return carry

        lax.fori_loop(0, HEADS_DEV, step, 0)

    def send_half(block, half, role, where):
        links.send(cot_all.at[block, half], cot_all.at[block, half], role, where, False)

    def halves(block, role):
        links.arrive(cot_all.at[block, low], role, y_down)
        links.arrive(cot_all.at[block, top], role + 1, y_up)

    project(part, first=True)
    each_head(lambda h: attend(h, OWN, first=True))
    links.arrive(cot_all.at[down], COT + 1, y_down)
    send_half(down, low, COT + 3, y_up)
    links.arrive(cot_all.at[up], COT + 2, y_up)
    send_half(up, top, COT + 4, y_down)
    send_heads(1)
    project(down)
    project(up)
    links.arrive(ids_all.at[0], IDS, before)
    links.arrive(ids_all.at[4], IDS + 1, after)
    links.send(ids_all.at[sum_slot], ids_all.at[sib_slot], IDS + 3, sibling)
    links.arrive(cot_all.at[over, low], COT, far)
    send_half(over, low, COT + 5, y_up)
    send_half(over, low, COT + 6, y_down)
    links.arrive(cot_all.at[over, top], COT + 9, far)
    send_half(over, top, COT + 10, y_up)
    send_half(over, top, COT + 11, y_down)
    project(over)
    send_heads(2)
    links.arrive(ids_all.at[sib_slot], IDS + 2, sibling)

    def attend_sibling(h):
        links.arrive(kv_all.at[sib_slot, :, :, head_columns(h)], KV + 4 * h + 2, sibling)
        attend(h, sib_slot)

    each_head(attend_sibling)
    halves(across, COT + 3)
    project(across)
    links.arrive(ids_all.at[relay_slot], IDS + 3, sibling)

    down_over, up_over, across_over = down + flip, up + flip, across + flip
    links.arrive(cot_all.at[down_over, low], COT + 5, y_down)
    send_half(down_over, low, COT + 7, y_up)
    links.arrive(cot_all.at[up_over, top], COT + 11, y_up)
    send_half(up_over, top, COT + 8, y_down)

    def rest_of_cotangent():
        links.arrive(cot_all.at[down_over, top], COT + 10, y_down)
        links.arrive(cot_all.at[up_over, low], COT + 6, y_up)
        project(down_over)
        project(up_over)
        halves(across_over, COT + 7)
        project(across_over)
        d_att[...] = d_acc[...].astype(BF16)

    planes = (0, flip)

    def share_plane(n):
        add = planes[n]
        role = MIX + 6 * n

        def mix(block):
            m_ref[block] = dot(att[...], w_ref[:, columns(block)], (1, 0)).astype(BF16)

        mix(across + add)
        links.send(m_ref.at[across + add, low], m_hop.at[n, 0], role, y_up, False)
        links.send(m_ref.at[across + add, top], m_hop.at[n, 1], role + 1, y_down, False)
        mix(up + add)
        links.send(m_ref.at[up + add, top], m_in.at[n, 0, top], role + 2, y_up, False)
        mix(down + add)
        links.send(m_ref.at[down + add, low], m_in.at[n, 1, low], role + 3, y_down, False)
        mix(part + add)

    def plane_hops(n):
        add = planes[n]
        role = MIX + 6 * n
        links.arrive(m_hop.at[n, 0], role, y_down)
        m_out[n, 0] = add_up(m_ref[up + add, low], m_hop[n, 0])
        links.send(m_out.at[n, 0], m_in.at[n, 0, low], role + 4, y_up, False)
        links.arrive(m_hop.at[n, 1], role + 1, y_up)
        m_out[n, 1] = add_up(m_ref[down + add, top], m_hop[n, 1])
        links.send(m_out.at[n, 1], m_in.at[n, 1, top], role + 5, y_down, False)

    def quarter(step):
        return lax.rem(x + step, 4)

    below, above, opposite = quarter(3), quarter(1), quarter(2)

    def weight_rows(h):
        rows = head_columns(h)

        def two_blocks(n, carry):
            for side in range(2):
                term = dot(att_t[rows, :], cot_all[2 * n + side], (1, 0)).astype(BF16)
                side_cols = pl.ds(side * COLS, COLS)
                for c in range(2):
                    for j in range(4):
                        first = (4 * c + j) * PIECE_ROWS
                        w_part[h, c, n, j, :, side_cols] = term[first : first + PIECE_ROWS]
            return carry

        lax.fori_loop(0, 4, two_blocks, 0)
        links.send(
            w_part.at[h, 1 - core], w_core.at[h], SUM + SUM_ROLES * h + CORE, sibling, False
        )

    def out_rows(h, c, first, count):
        start = h * HEAD + c * (HEAD // 2) + first * PIECE_ROWS
        return pl.ds(pl.multiple_of(start, PIECE_ROWS), count * PIECE_ROWS)

    def out_cols(block):
        return pl.ds(pl.multiple_of(block * PIECE_COLS, PIECE_COLS), PIECE_COLS)

    def add_up(*terms):
        return sum(t.astype(F32) for t in terms).astype(BF16)

    def sum_cores(h):
        role = SUM + SUM_ROLES * h
        links.arrive(w_core.at[h], role + CORE, sibling)

        def add(i, carry):
            w_sum[h, i] = add_up(w_part[h, core, i], w_core[h, i])
            return carry

        lax.fori_loop(0, 4, add, 0)
        role += XR
        links.send(w_sum.at[h, opposite, z_low], w_hop.at[h, 0], role, x_up, False)
        links.send(w_sum.at[h, opposite, z_top], w_hop.at[h, 1], role + 1, x_down, False)
        links.send(w_sum.at[h, above, z_top], w_in.at[h, 0, z_top], role + 2, x_up, False)
        links.send(w_sum.at[h, below, z_low], w_in.at[h, 1, z_low], role + 3, x_down, False)

    def sum_hops(h):
        role = SUM + SUM_ROLES * h + XR
        links.arrive(w_hop.at[h, 0], role, x_down)
        w_hop[h, 0] = add_up(w_sum[h, above, z_low], w_hop[h, 0])
        links.send(w_hop.at[h, 0], w_in.at[h, 0, z_low], role + 4, x_up, False)
        links.arrive(w_hop.at[h, 1], role + 1, x_up)
        w_hop[h, 1] = add_up(w_sum[h, below, z_top], w_hop[h, 1])
        links.send(w_hop.at[h, 1], w_in.at[h, 1, z_top], role + 5, x_down, False)

    def sum_x(h):
        role = SUM + SUM_ROLES * h + XR
        links.arrive(w_in.at[h, 0, z_top], role + 2, x_down)
        links.arrive(w_in.at[h, 1, z_low], role + 3, x_up)
        links.arrive(w_in.at[h, 0, z_low], role + 4, x_down)
        links.arrive(w_in.at[h, 1, z_top], role + 5, x_up)
        w_x[h] = add_up(w_sum[h, x], w_in[h, 0], w_in[h, 1])
        role = SUM + SUM_ROLES * h + ZR
        for d in range(3):
            links.send(w_x.at[h, lax.rem(z + d + 1, 4)], w_z.at[h, d], role + d, z_to[d], False)

    def sum_z(h):
        role = SUM + SUM_ROLES * h + ZR
        for d in range(3):
            links.arrive(w_z.at[h, d], role + d, z_from[d])
        mine = gw_ref.at[out_rows(h, core, z, 1), out_cols(x)]
        mine[...] = add_up(w_x[h, z], w_z[h, 0], w_z[h, 1], w_z[h, 2])
        role = SUM + SUM_ROLES * h + ZG
        for d in range(3):
            links.send(mine, mine, role + d, z_to[d], False)

    def spread_x(h):
        role = SUM + SUM_ROLES * h
        for d in range(3):
            rows = out_rows(h, core, lax.rem(z + 3 - d, 4), 1)
            links.arrive(gw_ref.at[rows, out_cols(x)], role + ZG + d, z_from[d])
        mine = gw_ref.at[out_rows(h, core, 0, 4), out_cols(x)]
        links.send(mine, mine, role + XG, x_up, False)
        links.send(mine, mine, role + XG + 1, x_down, False)
        links.send(mine, mine, role + CG, sibling, False)

    def spread_on(h):
        role = SUM + SUM_ROLES * h
        for n, (block, back_from, on_to) in enumerate(((below, x_down, x_up), (above, x_up, x_down))):
            whole = gw_ref.at[out_rows(h, core, 0, 4), out_cols(block)]
            part_of = gw_ref.at[out_rows(h, core, 2 * n, 2), out_cols(block)]
            links.arrive(whole, role + XG + n, back_from)
            links.send(part_of, part_of, role + XG + 2 + n, on_to, False)
            links.send(whole, whole, role + CG + 1 + n, sibling, False)

    def spread_cores(h):
        role = SUM + SUM_ROLES * h
        for n, back_from in enumerate((x_down, x_up)):
            part_of = gw_ref.at[out_rows(h, core, 2 * n, 2), out_cols(opposite)]
            links.arrive(part_of, role + XG + 2 + n, back_from)
        whole = gw_ref.at[out_rows(h, core, 0, 4), out_cols(opposite)]
        links.send(whole, whole, role + CG + 3, sibling, False)

    def spread_done(h):
        role = SUM + SUM_ROLES * h + CG
        for n, block in enumerate((x, below, above, opposite)):
            links.arrive(gw_ref.at[out_rows(h, 1 - core, 0, 4), out_cols(block)], role + n, sibling)

    def sum_left(h):
        role = SUM + SUM_ROLES * h
        links.left(w_core.at[h], role + CORE, sibling)
        for n in range(6):
            links.left(w_hop.at[h, 0], role + XR + n, x_up)
        for n in range(3):
            links.left(w_z.at[h, n], role + ZR + n, z_to[n])
            links.left(w_z.at[h, n], role + ZG + n, z_to[n])
        whole = gw_ref.at[out_rows(h, core, 0, 4), out_cols(x)]
        half = gw_ref.at[out_rows(h, core, 0, 2), out_cols(x)]
        for n in range(2):
            links.left(whole, role + XG + n, x_up)
            links.left(half, role + XG + 2 + n, x_up)
        for n in range(4):
            links.left(whole, role + CG + n, sibling)

    final = HEADS_DEV - 1

    def per_head(h):
        def of_last(step):
            pl.when(h > 0)(lambda: step(h - 1))

        cols = head_columns(h)
        role = KV + 4 * h
        links.arrive(kv_all.at[0, :, :, cols], role, before)
        links.arrive(kv_all.at[4, :, :, cols], role + 1, after)
        links.send(
            kv_all.at[sum_slot, :, :, cols], kv_all.at[sib_slot, :, :, cols], role + 3, sibling,
            False,
        )
        attend(h, 0)
        attend(h, 4)
        pl.when(h == 0)(rest_of_cotangent)
        links.arrive(kv_all.at[relay_slot, :, :, cols], role + 3, sibling)
        attend(h, relay_slot)
        settle(h)
        weight_rows(h)
        pl.when(h == final)(lambda: share_plane(1))
        role = DKV + 4 * h
        back(h, relay_slot, first=True)
        links.send(
            dkv.at[relay_slot, :, :, cols], dkv_in.at[1, :, :, cols], role + 1, sibling, False
        )
        sum_cores(h)
        back(h, direct_slot)
        links.send(
            dkv.at[direct_slot, :, :, cols], dkv_in.at[2 + core, :, :, cols], role + 2 + core,
            direct_to, False,
        )
        back(h, sum_slot)
        links.arrive(dkv_in.at[1, :, :, cols], role + 1, sibling)
        for n in range(2):
            dkv[sum_slot, n, :, cols] = add_up(
                dkv[sum_slot, n, :, cols], dkv_in[1, n, :, cols]
            )
        links.send(
            dkv.at[sum_slot, :, :, cols], dkv_in.at[3 - core, :, :, cols], role + 3 - core,
            sum_to, False,
        )
        sum_hops(h)
        back(h, sib_slot)
        links.send(dkv.at[sib_slot, :, :, cols], dkv_in.at[0, :, :, cols], role, sibling, False)
        pl.when(h == final)(lambda: plane_hops(1))
        back(h, OWN, last=True)
        sum_x(h)
        of_last(sum_z)

    each_head(per_head)

    def along_y(n):
        add = planes[n]
        role = MIX + 6 * n
        links.arrive(m_in.at[n, 0, top], role + 2, y_down)
        links.arrive(m_in.at[n, 1, low], role + 3, y_up)
        links.arrive(m_in.at[n, 0, low], role + 4, y_down)
        links.arrive(m_in.at[n, 1, top], role + 5, y_up)
        return add_up(m_ref[part + add], m_in[n, 0], m_in[n, 1])

    def add_keys(h):
        cols = head_columns(h)
        role = DKV + 4 * h
        links.arrive(dkv_in.at[0, :, :, cols], role, sibling)
        links.arrive(dkv_in.at[2, :, :, cols], role + 2, after)
        links.arrive(dkv_in.at[3, :, :, cols], role + 3, before)
        for n, out in enumerate((gk_ref, gv_ref)):
            out[:, cols] = add_up(
                own[n, :, cols], dkv_in[0, n, :, cols], dkv_in[2, n, :, cols],
                dkv_in[3, n, :, cols],
            )

    share_plane(0)
    sum_z(final)
    spread_x(0)
    spread_x(1)
    plane_hops(0)
    spread_x(final)
    m_far[0] = along_y(1)
    links.send(m_far.at[0], m_far.at[1], FAR, far)
    spread_on(0)
    spread_on(1)
    spread_cores(0)
    spread_cores(1)
    spread_on(final)
    m_in[0, 0] = along_y(0)
    spread_cores(final)
    each_head(add_keys)
    links.arrive(m_far.at[1], FAR, far)
    mixed_ref[...] = add_up(m_in[0, 0], m_far[1])
    each_head(spread_done)

    def heads_left(h):
        cols = head_columns(h)
        for n in range(4):
            links.left(kv_all.at[OWN, :, :, cols], KV + 4 * h + n, sibling)
            links.left(dkv.at[OWN, :, :, cols], DKV + 4 * h + n, sibling)
        sum_left(h)

    each_head(heads_left)
    for n in range(2):
        for k in range(6):
            links.left(m_hop.at[n, 0], MIX + 6 * n + k, y_up)
    for role in (3, 4, 5, 6, 7, 8, 10, 11):
        links.left(cot_all.at[0, low], COT + role, y_up)
    links.finish()


def sublayer(ids, query, keys, values, cotangent, weight):
    block = (ROWS, COLS)
    bf16 = lambda *shape: pltpu.VMEM(shape, BF16)
    f32 = lambda *shape: pltpu.VMEM(shape, F32)
    heads = (HEADS_DEV, ROWS, HEAD)
    piece = (PIECE_ROWS, PIECE_COLS)
    return pl.pallas_call(
        sublayer_kernel,
        out_shape=tuple([jax.ShapeDtypeStruct(block, BF16)] * 4)
        + (jax.ShapeDtypeStruct((COLS, FEATURES), BF16),),
        in_specs=[VMEM] * 6,
        out_specs=(VMEM,) * 5,
        scratch_shapes=[
            pltpu.VMEM((WINDOW, 1, ROWS), jnp.int32),
            pltpu.VMEM((ROWS, 128), jnp.int32),
            bf16(WINDOW, 2, *block),
            bf16(TP, *block),
            bf16(*block),
            f32(*block),
            f32(*heads),
            f32(*heads),
            f32(*heads),
            f32(ROWS, HEAD),
            f32(ROWS, HEAD),
            f32(ROWS, HEAD),
            bf16(*block),
            bf16(COLS, ROWS),
            bf16(WINDOW, 2, *block),
            f32(2, *block),
            bf16(4, 2, *block),
            bf16(TP, *block),
            bf16(2, 2, HALF, COLS),
            bf16(2, 2, *block),
            bf16(2, 2, HALF, COLS),
            bf16(2, *block),
            bf16(HEADS_DEV, 2, 4, 4, *piece),
            bf16(HEADS_DEV, 4, 4, *piece),
            bf16(HEADS_DEV, 4, 4, *piece),
            bf16(HEADS_DEV, 2, 2, *piece),
            bf16(HEADS_DEV, 2, 4, *piece),
            bf16(HEADS_DEV, 4, *piece),
            bf16(HEADS_DEV, 3, *piece),
            pltpu.SemaphoreType.DMA((ROLES,)),
            pltpu.SemaphoreType.DMA((ROLES,)),
        ],
        compiler_params=pltpu.CompilerParams(
            collective_id=0, has_side_effects=True, vmem_limit_bytes=LIMIT
        ),
        name="sublayer",
    )(ids, query, keys, values, cotangent, weight)


def hand_over_kernel(*refs):
    count = len(refs) // 2
    for n in range(count):
        refs[count + n][...] = refs[n][...]


def hand_over(arrays):
    return pl.pallas_call(
        hand_over_kernel,
        out_shape=tuple(jax.ShapeDtypeStruct(a.shape, a.dtype) for a in arrays),
        in_specs=[VMEM] * len(arrays),
        out_specs=(VMEM,) * len(arrays),
        name="hand_over",
    )(*arrays)


def on_device(query, keys, values, image_ids, out_weight, cotangent):
    return hand_over(sublayer(image_ids, query, keys, values, cotangent, out_weight))


def solution(mesh):
    placed = (
        P("ctx", "tp"),
        P("ctx", "tp"),
        P("ctx", "tp"),
        P("ctx"),
        P("tp", None),
        P("ctx", "tp"),
    )
    return jax.shard_map(
        on_device,
        mesh=mesh,
        in_specs=placed,
        out_specs=(P("ctx", "tp"), P("ctx", "tp"), P("ctx", "tp"), P("ctx", "tp"), P("tp", None)),
        check_vma=False,
    )
```
